256 devices in a mesh: grp: 4 (over x), ctx: 64 (over z, y, core).
Axes of the slice: x: 4, y: 4, z: 8, core: 2. Of those that a mesh axis runs over, the one named last changes fastest.
Arguments:
- queries: bfloat16 [32, 4, 16384], P('grp', None, 'ctx'), may hold values from -8 to 8
- prefix_kv: bfloat16 [8, 65536, 2048], P('grp', 'ctx'), may hold values from -16 to 16
- suffix_kv: bfloat16 [32, 1024, 2048], P('grp', 'ctx'), may hold values from -24 to 24
- new_kv: bfloat16 [32, 4, 2048], P('grp'), may hold values from -24 to 24
- prefix_id: int32 [32, 1], P('grp'), may hold values from 0 to 7; in each aligned block of 8 rows (0 to 7, 8 to 15, ...) at most 2 rows name the same one
- place: int32 [8], replicated, may hold values from 0 to 7, each once
- suffix_len: int32 [32], P('grp'), may hold values from 1 to 1024, 16384 in all
Outputs:
- attended: bfloat16 [32, 4, 16384], P('grp', None, 'ctx')
The draws below stay inside these ranges and needn't reach their ends.
Inputs may be any that keep to these rules, and one draw needn't show every extreme that they name: `prefix_id`: among the 8 requests of one index of grp, at most 2 name the same prefix; some prefix is named by exactly 2 of them. `suffix_len`: some request has exactly 1024 cached positions.
All inputs are finite; a program needn't handle non-finite values. No bound on the sum of `suffix_len` on one device may be relied on, other than what follows from the above.
Results may differ from the reference program's by a relative error of at most 0.014.
Values may be sent and summed in bfloat16 or wider, within the bound.
No kernel may reach another device: no remote copies, remote signals or barrier semaphores. Data moves between devices by JAX's collectives and lax.ppermute only.
A program may use at most 320 MiB of HBM per device.

```python
import math
import jax
import jax.numpy as jnp
import numpy as np
from jax import lax

HQ = 128
KVH = 8
HD = 128
STEPS = 4
R_G = 8
PREFIXES = 8
M = 2
REQUESTS = 32
PREF_LEN = 65536
SUF = 1024


def sign_pattern(width):
    return 1.0 - 2.0 * (jnp.arange(width) % 2).astype(jnp.float32)


def key_block(key, rows, span, low, high, rate):
    base = jnp.clip(jax.random.normal(jax.random.fold_in(key, 1), (rows, span, 2, KVH, HD), jnp.float32), -5.0, 5.0)
    scales = jnp.exp(jax.random.uniform(jax.random.fold_in(key, 2), (rows, span, 1, KVH, 1), jnp.float32, math.log(low), math.log(high)))
    picked = jax.random.uniform(jax.random.fold_in(key, 3), (rows, span, 1, 1, 1), jnp.float32) < rate
    strength = jax.random.uniform(jax.random.fold_in(key, 4), (rows, span, 1, 1, 1), jnp.float32, 3.96, 4.0)
    keys = base[:, :, :1] * scales + jnp.where(picked, strength, 0.0) * sign_pattern(HD)
    values = base[:, :, 1:]
    return jnp.concatenate([keys, values], axis=2).reshape(rows, span, 2 * KVH * HD)


def draw_queries(key, part):
    key = jax.random.fold_in(key, 5)
    base = jnp.clip(jax.random.normal(jax.random.fold_in(key, 1), (REQUESTS, STEPS, HQ * HD), jnp.float32), -5.0, 5.0)
    return base.astype(jnp.bfloat16)


def draw_prefix_kv(key, part):
    key = jax.random.fold_in(key, 11)
    rate = 0.0
    return key_block(key, PREFIXES, PREF_LEN, 0.3, 2.0, rate).astype(jnp.bfloat16)


def draw_suffix_kv(key, part):
    key = jax.random.fold_in(key, 17)
    return key_block(key, REQUESTS, SUF, 0.5, 4.0, 0.0).astype(jnp.bfloat16)


def draw_new_kv(key, part):
    key = jax.random.fold_in(key, 23)
    return key_block(key, REQUESTS, STEPS, 0.5, 4.0, 0.0).astype(jnp.bfloat16)


def length_profile(count, total, most, lean):
    portions = [(1 << 20) // math.isqrt(grade ** lean) + 1 for grade in range(2, count + 1)]
    spare, counts = total - most - (count - 1), [1] * (count - 1)
    while spare > 0:
        free = [i for i in range(count - 1) if counts[i] < most]
        mass, remaining = sum([portions[i] for i in free]), spare
        for i in free:
            addition = min(most - counts[i], max(1, remaining * portions[i] // mass), spare)
            counts[i] = counts[i] + addition
            spare = spare - addition
    return np.array([most] + counts)


def ragged(stream_key, count, total, limit, lean):
    if count == 2:
        one = jax.random.randint(stream_key, (), max(1, total - limit), min(limit, total - 1) + 1)
        return jnp.stack([one, total - one])
    lengths = jnp.asarray(length_profile(count, total, limit, lean), jnp.int32)
    couples = (count - 1) // 2
    donor, receiver = lengths[1:1 + 2 * couples:2], lengths[2:2 + 2 * couples:2]
    margin = jnp.minimum(donor - 1, limit - receiver)
    shifted = jax.random.randint(jax.random.fold_in(stream_key, 1), (couples,), 0, 1 << 20) % (margin + 1)
    lengths = lengths.at[1:1 + 2 * couples:2].set(donor - shifted).at[2:2 + 2 * couples:2].set(receiver + shifted)
    return lengths[jax.random.permutation(jax.random.fold_in(stream_key, 2), count)]


def shared_out(own_key, own, number, rows, amount, top, bound, slope):
    sequence = jax.random.permutation(own_key, amount)
    crowded, ordinary = portions_of(amount, rows * top, bound, slope, True), portions_of(amount, rows * top, bound, slope, False)
    places = jnp.arange(amount)

    def named(lengths, turn):
        used = int((lengths > 0).sum())
        fixed = max(1, used // 4)
        passed = fixed + (places - fixed + turn * (used - fixed)) % max(1, amount - fixed)
        return jnp.zeros((amount,), jnp.int32).at[sequence[jnp.where(places < fixed, places, passed)]].set(jnp.asarray(lengths, jnp.int32))

    lengths = jnp.where(number % 4 == 0, named(crowded, number // 4), named(ordinary, number - number // 4 - 1))
    mixed = jax.random.permutation(jax.random.fold_in(own, 3), amount)
    donor, receiver = mixed[0:amount // 2 * 2:2], mixed[1:amount // 2 * 2:2]
    room = jnp.minimum(lengths[donor] - 1, bound - lengths[receiver]) // 2
    room = jnp.where((donor == sequence[0]) | (receiver == sequence[0]) | (lengths[receiver] == 0), 0, jnp.maximum(room, 0))
    passed = jax.random.randint(jax.random.fold_in(own, 4), (amount // 2,), 0, 1 << 20) % (room + 1)
    lengths = lengths.at[donor].add(-passed).at[receiver].add(passed)
    labels = jnp.searchsorted(jnp.cumsum(lengths), jnp.arange(rows * top), side="right").astype(jnp.int32)
    table = labels.reshape(top, rows).T
    table = table[jax.random.permutation(jax.random.fold_in(own, 1), rows)]
    turn = jax.random.randint(jax.random.fold_in(own, 2), (rows, 1), 0, top)
    return jnp.take_along_axis(table, (jnp.arange(top)[None, :] + turn) % top, axis=1)


def portions_of(number_of, total, most, skew, full):
    weights = [(1 << 20) // math.isqrt(grade ** skew) + 1 for grade in range(1, number_of + 1)]
    largest = most if full else min(most, max(-(-total // number_of), total * weights[0] // sum(weights)))
    least = 1 if total - largest >= number_of - 1 else 0
    counts, spare = [largest] + [least] * (number_of - 1), total - largest - least * (number_of - 1)
    while spare > 0:
        movable = [i for i in range(1, number_of) if counts[i] < largest] or [i for i in range(1, number_of) if counts[i] < most]
        whole, remaining = sum([weights[i] for i in movable]), spare
        for i in movable:
            addition = min(most - counts[i], max(1, remaining * weights[i] // whole), spare)
            counts[i] = counts[i] + addition
            spare = spare - addition
    return np.array(counts)


def setup_inputs(seed: int = 0) -> dict:
    key_of = jax.random.split(jax.random.key(seed), 8)
    queries = draw_queries(jax.random.fold_in(key_of[7], 71), 0)
    prefix_kv = draw_prefix_kv(jax.random.fold_in(key_of[7], 71), 0)
    suffix_kv = draw_suffix_kv(jax.random.fold_in(key_of[7], 71), 0)
    new_kv = draw_new_kv(jax.random.fold_in(key_of[7], 71), 0)
    prefix_id_keys = jax.random.split(jax.random.fold_in(key_of[4], 1), REQUESTS // R_G)
    prefix_id_turns = jax.random.permutation(jax.random.fold_in(key_of[4], 3), REQUESTS // R_G)
    prefix_id = jax.vmap(lambda own, number: shared_out(jax.random.fold_in(key_of[4], 2), own, number, R_G, PREFIXES, 1, M, 2))(prefix_id_keys, prefix_id_turns).reshape((REQUESTS, 1))
    place = jax.random.permutation(key_of[5], PREFIXES).astype(jnp.int32)
    suffix_len = ragged(key_of[6], REQUESTS, REQUESTS * SUF // 2, SUF, 2).astype(jnp.int32)
    return {"queries": queries, "prefix_kv": prefix_kv, "suffix_kv": suffix_kv, "new_kv": new_kv, "prefix_id": prefix_id, "place": place, "suffix_len": suffix_len}


neg_big = -1.0e30


def reference(queries, prefix_kv, suffix_kv, new_kv, prefix_id, place, suffix_len):
    scale = HD ** -0.5
    width = KVH * HD
    share = HQ // KVH

    def one_request(items):
        query, chosen, suffix, fresh, length = items
        row = place[chosen[0]].astype(jnp.int32)
        stored = lax.dynamic_index_in_dim(prefix_kv, row, 0, keepdims=False)
        joined = jnp.concatenate([stored, suffix, fresh], axis=0).astype(jnp.float32)
        keys = joined[:, :width].reshape(-1, KVH, HD)
        values = joined[:, width:].reshape(-1, KVH, HD)
        shaped = query.astype(jnp.float32).reshape(STEPS, KVH, share, HD)
        scores = jnp.einsum("skgd,tkd->skgt", shaped, keys) * scale
        count = keys.shape[0]
        where_t = jnp.arange(count, dtype=jnp.int32)
        plen = stored.shape[0]
        slen = suffix.shape[0]
        steps_at = jnp.arange(STEPS, dtype=jnp.int32)
        is_pref = where_t < plen
        is_suf = (where_t >= plen) & (where_t < plen + slen) & ((where_t - plen) < length)
        is_new = (where_t >= plen + slen)[None, :] & ((where_t - plen - slen)[None, :] <= steps_at[:, None])
        valid = (is_pref | is_suf)[None, :] | is_new
        valid = valid[:, None, None, :]
        masked = jnp.where(valid, scores, neg_big)
        top = jnp.max(masked, axis=-1)
        weights = jnp.where(valid, jnp.exp(masked - top[..., None]), 0.0)
        total = jnp.sum(weights, axis=-1)
        rounded = weights.astype(jnp.bfloat16).astype(jnp.float32)
        summed = jnp.einsum("skgt,tkd->skgd", rounded, values)
        result = summed / total[..., None]
        return result.reshape(STEPS, HQ * HD).astype(jnp.bfloat16)

    return lax.map(one_request, (queries, prefix_id, suffix_kv, new_kv, suffix_len))
```

```python
import functools

import jax
import jax.numpy as jnp
from jax import lax
from jax.experimental import pallas as pl
from jax.experimental.pallas import tpu as pltpu
from jax.sharding import Mesh
from jax.sharding import PartitionSpec as P

GRP, NZ, NY, NC = 4, 8, 4, 2
HD = 128
STEPS = 4
REQ = 8
SPAN = 16
HALF = 1024
SLAB = 144
TAIL = 32
ROWS = NZ * SLAB + TAIL
BACK = 40
FACTOR = HD ** (-0.5) * 1.4426950408889634
NEG = -1e30
F32 = jnp.float32
BF16 = jnp.bfloat16
VMEM_LIMIT = 56 * 1024 * 1024


def nt_dot(a, b):
    return lax.dot_general(a, b, (((1,), (1,)), ((), ())), preferred_element_type=F32)


def tn_dot(a, b):
    return lax.dot_general(a, b, (((0,), (0,)), ((), ())), preferred_element_type=F32)


def whole(shape, space=pltpu.VMEM):
    return pl.BlockSpec(memory_space=space)


def slot_of(r, pid_ref, place_ref):
    chosen = [place_ref[pid_ref[i, 0]] for i in range(r + 1)]
    rank = jnp.int32(0)
    for i in range(r):
        rank = rank + (chosen[i] == chosen[r]).astype(jnp.int32)
    return chosen[r] * 2 + rank


def pack_queries_kernel(pid_ref, place_ref, q_ref, send_ref, rows_ref, buf):
    buf[...] = jnp.zeros_like(buf)
    for pair in range(REQ // 2):
        both = []
        for r in (2 * pair, 2 * pair + 1):
            q = q_ref[r].astype(F32)
            rows = jnp.concatenate([q[:, :HD], q[:, HD:]], axis=0)
            buf[slot_of(r, pid_ref, place_ref)] = rows
            both.append(rows)
        rows_ref[pair] = jnp.concatenate(both, axis=0).astype(BF16)
    for g in range(GRP):
        block = buf[4 * g : 4 * g + 4].reshape(32, HD).astype(BF16)
        for z in range(NZ):
            send_ref[g * NZ + z] = block


def pack_queries(prefix_id, place, queries):
    return pl.pallas_call(
        pack_queries_kernel,
        out_shape=(
            jax.ShapeDtypeStruct((GRP * NZ, 32, HD), BF16),
            jax.ShapeDtypeStruct((REQ // 2, 16, HD), BF16),
        ),
        in_specs=[
            pl.BlockSpec(memory_space=pltpu.SMEM),
            pl.BlockSpec(memory_space=pltpu.SMEM),
            pl.BlockSpec(memory_space=pltpu.VMEM),
        ],
        out_specs=(
            pl.BlockSpec(memory_space=pltpu.VMEM),
            pl.BlockSpec(memory_space=pltpu.VMEM),
        ),
        scratch_shapes=[pltpu.VMEM((16, 8, HD), F32)],
        name="pack_queries",
    )(prefix_id, place, queries)


def pack_suffix_kernel(kv_ref, out_ref):
    for z in range(NZ):
        for y in range(NY):
            for r in range(2):
                out_ref[z * NY + y, r, :, :HD] = kv_ref[2 * y + r, :, z * HD : (z + 1) * HD]
                out_ref[z * NY + y, r, :, HD:] = kv_ref[
                    2 * y + r, :, (NZ + z) * HD : (NZ + z + 1) * HD
                ]


def pack_suffix(suffix_kv):
    return pl.pallas_call(
        pack_suffix_kernel,
        out_shape=jax.ShapeDtypeStruct((NZ * NY, 2, SPAN, 2 * HD), BF16),
        in_specs=[pl.BlockSpec(memory_space=pltpu.VMEM)],
        out_specs=pl.BlockSpec(memory_space=pltpu.VMEM),
        name="pack_suffix",
    )(suffix_kv)


def split_total(total):
    high = total.astype(BF16).astype(F32)
    return high, total - high


def prefix_kernel(q0, q1, q2, q3, ka, kb, va, vb, o0, o1, o2, o3):
    sums, stats = [], []
    for p in range(2):
        q = jnp.concatenate(
            [ref[:, 0, p * 16 : (p + 1) * 16, :].reshape(64, HD) for ref in (q0, q1, q2, q3)],
            axis=0,
        )
        sa = nt_dot(ka[p], q) * FACTOR
        sb = nt_dot(kb[p], q) * FACTOR
        top = jnp.maximum(jnp.max(sa, axis=0, keepdims=True), jnp.max(sb, axis=0, keepdims=True))
        top = top.astype(BF16).astype(F32)
        wa = jnp.exp2(sa - top)
        wb = jnp.exp2(sb - top)
        total = jnp.sum(wa, axis=0, keepdims=True) + jnp.sum(wb, axis=0, keepdims=True)
        summed = tn_dot(va[p], wa.astype(BF16)) + tn_dot(vb[p], wb.astype(BF16))
        high, low = split_total(total)
        row = lax.broadcasted_iota(jnp.int32, (16, 256), 0)
        stat = jnp.where(row == 0, top, jnp.where(row == 1, high, jnp.where(row == 2, low, 0.0)))
        sums.append(summed)
        stats.append(stat)
    for k, out in enumerate((o0, o1, o2, o3)):
        cols = slice(64 * k, 64 * (k + 1))
        out[:HD, :] = jnp.concatenate([sums[0][:, cols], sums[1][:, cols]], axis=1).astype(BF16)
        out[HD:, :] = jnp.concatenate([stats[0][:, cols], stats[1][:, cols]], axis=1).astype(BF16)


def prefix_attention(gathered, own, other):
    q_spec = pl.BlockSpec((GRP, 1, 32, HD), lambda z: (0, z, 0, 0))
    k_spec = pl.BlockSpec((2, HALF, HD), lambda z: (0, 0, z))
    v_spec = pl.BlockSpec((2, HALF, HD), lambda z: (0, 0, NZ + z))
    out_spec = pl.BlockSpec((SLAB, HD), lambda z: (z, 0))
    return pl.pallas_call(
        prefix_kernel,
        grid=(NZ,),
        out_shape=(jax.ShapeDtypeStruct((ROWS, HD), BF16),) * NY,
        in_specs=[q_spec] * 4 + [k_spec, k_spec, v_spec, v_spec],
        out_specs=(out_spec,) * NY,
        compiler_params=pltpu.CompilerParams(vmem_limit_bytes=VMEM_LIMIT),
        cost_estimate=pl.CostEstimate(
            flops=4 * 4096 * 2048 * HD, bytes_accessed=18 << 20, transcendentals=4096 * 2048
        ),
        name="prefix_attention",
    )(*gathered, own, other, own, other)


def suffix_kernel(
    at_ref, len_ref, q0, q1, q2, q3, kv_own, kv_other, new_k, new_v, i0, i1, i2, i3, o0, o1, o2, o3
):
    y, core = at_ref[0], at_ref[2]
    index = lax.broadcasted_iota(jnp.int32, (32, 512), 1)
    base = (index // SPAN) * (2 * SPAN) + index % SPAN
    step = lax.broadcasted_iota(jnp.int32, (32, 1), 0) % STEPS
    sums, tops, totals = [], [], []
    queries = [ref[0].astype(F32) for ref in (q0, q1, q2, q3)]
    for r in range(2):
        length = len_ref[2 * y + r]
        qf = jnp.concatenate([q[8 * r : 8 * r + 8] for q in queries], axis=0)
        q = qf.astype(BF16)
        scores = []
        for ref, c in ((kv_own, core), (kv_other, 1 - core)):
            s = nt_dot(q, ref[:, r, :, :HD].reshape(512, HD)) * FACTOR
            scores.append(jnp.where(base + c * SPAN < length, s, NEG))
        kn, vn = new_k[r].astype(F32), new_v[r].astype(F32)
        fresh = []
        for t in range(STEPS):
            s = jnp.sum(qf * kn[t : t + 1], axis=1, keepdims=True) * FACTOR
            fresh.append(jnp.where(step >= t, s, NEG))
        top = functools.reduce(
            jnp.maximum, [jnp.max(s, axis=1, keepdims=True) for s in scores] + fresh
        )
        top = top.astype(BF16).astype(F32)
        total = jnp.zeros((32, 1), F32)
        summed = jnp.zeros((32, HD), F32)
        for s, ref in zip(scores, (kv_own, kv_other)):
            w = jnp.exp2(s - top)
            total = total + jnp.sum(w, axis=1, keepdims=True)
            summed = summed + jnp.dot(
                w.astype(BF16), ref[:, r, :, HD:].reshape(512, HD), preferred_element_type=F32
            )
        for t in range(STEPS):
            w = jnp.exp2(fresh[t] - top)
            total = total + w
            summed = summed + w.astype(BF16).astype(F32) * vn[t : t + 1]
        sums.append(summed)
        tops.append(top)
        totals.append(total)
    lane = lax.broadcasted_iota(jnp.int32, (16, HD), 1)
    for k, out in enumerate((o0, o1, o2, o3)):
        rows = slice(8 * k, 8 * k + 8)
        top = jnp.concatenate([t[rows] for t in tops], axis=0)
        high, low = split_total(jnp.concatenate([t[rows] for t in totals], axis=0))
        out[:16, :] = jnp.concatenate([s[rows] for s in sums], axis=0).astype(BF16)
        stat = jnp.where(
            lane == 0, top, jnp.where(lane == 1, high, jnp.where(lane == 2, low, 0.0))
        )
        out[16:, :] = stat.astype(BF16)


def suffix_attention(at, lengths, queries, kv_own, kv_other, new_kv, partials):
    q_spec = pl.BlockSpec((1, 16, HD), lambda i, at, n: (at[0], 0, 0))
    kv_spec = pl.BlockSpec((NZ * NY, 2, SPAN, 2 * HD), lambda i, at, n: (0, 0, 0, 0))
    new_specs = [
        pl.BlockSpec((2, STEPS, HD), lambda i, at, n: (at[0], 0, at[1])),
        pl.BlockSpec((2, STEPS, HD), lambda i, at, n: (at[0], 0, NZ + at[1])),
    ]
    tail_spec = pl.BlockSpec((TAIL, HD), lambda i, at, n: (NZ * SLAB // TAIL, 0))
    return pl.pallas_call(
        suffix_kernel,
        grid_spec=pltpu.PrefetchScalarGridSpec(
            num_scalar_prefetch=2,
            grid=(1,),
            in_specs=[q_spec] * 4 + [kv_spec, kv_spec] + new_specs + [tail_spec] * 4,
            out_specs=[tail_spec] * 4,
        ),
        out_shape=[jax.ShapeDtypeStruct((ROWS, HD), BF16)] * NY,
        input_output_aliases={10 + k: k for k in range(4)},
        compiler_params=pltpu.CompilerParams(vmem_limit_bytes=VMEM_LIMIT),
        name="suffix_attention",
    )(at, lengths, *queries, kv_own, kv_other, new_kv, new_kv, *partials)


def combine_kernel(p0, p1, p2, p3, out_ref):
    for z in range(NZ):
        slabs = [ref[z * SLAB : (z + 1) * SLAB].astype(F32) for ref in (p0, p1, p2, p3)]
        tops = [s[HD : HD + 1] for s in slabs]
        top = functools.reduce(jnp.maximum, tops)
        factors = [jnp.exp2(t - top) for t in tops]
        summed = sum(s[:HD] * f for s, f in zip(slabs, factors))
        total = sum((s[HD + 1 : HD + 2] + s[HD + 2 : HD + 3]) * f for s, f in zip(slabs, factors))
        high, low = split_total(total)
        row = lax.broadcasted_iota(jnp.int32, (8, HD), 0)
        stat = jnp.where(row == 0, top, jnp.where(row == 1, high, jnp.where(row == 2, low, 0.0)))
        turned = jnp.transpose(summed)
        for g in range(GRP):
            out_ref[g * NZ + z] = jnp.concatenate(
                [turned[16 * g : 16 * g + 16], turned[64 + 16 * g : 80 + 16 * g], stat], axis=0
            ).astype(BF16)


def combine(parts):
    spec = pl.BlockSpec(memory_space=pltpu.VMEM)
    return pl.pallas_call(
        combine_kernel,
        out_shape=jax.ShapeDtypeStruct((GRP * NZ, BACK, HD), BF16),
        in_specs=[spec] * 4,
        out_specs=spec,
        name="combine",
    )(*parts)


def finish_kernel(at_ref, pid_ref, place_ref, back_ref, t0, t1, t2, t3, out_ref, turned, sums, tops, totals, tails):
    y, g = at_ref[0], at_ref[3]
    for half in range(2):
        stats = [
            back_ref[half * 16 + s].astype(F32)[32:BACK] for s in range(16)
        ]
        turned[half] = jnp.transpose(jnp.concatenate(stats, axis=0))
    for k, ref in enumerate((t0, t1, t2, t3)):
        tails[k] = ref[...].astype(F32)
    low_rows = pl.ds(pl.multiple_of(16 * g, 16), 16)
    high_rows = pl.ds(pl.multiple_of(64 + 16 * g, 16), 16)
    for src in range(GRP):
        cols = jnp.concatenate(
            [turned[src // 2, low_rows, :], turned[src // 2, high_rows, :]], axis=0
        )
        first = (src % 2) * 64
        col = [[cols[:, first + 8 * z + i : first + 8 * z + i + 1] for i in range(3)] for z in range(NZ)]
        top = functools.reduce(jnp.maximum, [c[0] for c in col])
        total = jnp.zeros((32, 1), F32)
        summed = jnp.zeros((32, HD), F32)
        for z in range(NZ):
            factor = jnp.exp2(col[z][0] - top)
            total = total + (col[z][1] + col[z][2]) * factor
            summed = summed + back_ref[src * NZ + z].astype(F32)[:32] * factor
        sums[4 * src : 4 * src + 4] = summed.reshape(4, 8, HD)
        tops[4 * src : 4 * src + 4] = jnp.broadcast_to(top, (32, HD)).reshape(4, 8, HD)
        totals[4 * src : 4 * src + 4] = jnp.broadcast_to(total, (32, HD)).reshape(4, 8, HD)
    for r in range(REQ):
        slot = slot_of(r, pid_ref, place_ref)
        k = (r // 2 + NY - y) % NY
        tail = tails[k]
        base = 8 * (r % 2)
        s_sum = tail[base : base + 8]
        stat = tail[16 + base : 24 + base]
        s_top, s_total = stat[:, 0:1], stat[:, 1:2] + stat[:, 2:3]
        p_sum, p_top, p_total = sums[slot], tops[slot], totals[slot]
        top = jnp.maximum(p_top, s_top)
        left, right = jnp.exp2(p_top - top), jnp.exp2(s_top - top)
        result = (p_sum * left + s_sum * right) / (p_total * left + s_total * right)
        out_ref[r] = jnp.concatenate([result[:STEPS], result[STEPS:]], axis=1).astype(BF16)


def finish(at, prefix_id, place, back, parts):
    smem = pl.BlockSpec(memory_space=pltpu.SMEM)
    spec = pl.BlockSpec((GRP * NZ, BACK, HD), lambda i: (0, 0, 0))
    tail_spec = pl.BlockSpec((TAIL, HD), lambda i: (NZ * SLAB // TAIL, 0))
    return pl.pallas_call(
        finish_kernel,
        grid=(1,),
        out_shape=jax.ShapeDtypeStruct((REQ, STEPS, 2 * HD), BF16),
        in_specs=[smem, smem, smem, spec] + [tail_spec] * 4,
        out_specs=pl.BlockSpec((REQ, STEPS, 2 * HD), lambda i: (0, 0, 0)),
        scratch_shapes=[
            pltpu.VMEM((2, HD, HD), F32),
            pltpu.VMEM((16, 8, HD), F32),
            pltpu.VMEM((16, 8, HD), F32),
            pltpu.VMEM((16, 8, HD), F32),
            pltpu.VMEM((NY, TAIL, HD), F32),
        ],
        name="finish",
    )(at, prefix_id, place, back, *parts)


def turn(x, by):
    return lax.ppermute(x, "y", [(i, (i + by) % NY) for i in range(NY)])


def swap(x):
    return lax.ppermute(x, "c", [(0, 1), (1, 0)])


def per_device(queries, prefix_kv, suffix_kv, new_kv, prefix_id, place, suffix_len):
    y = lax.axis_index("y")
    z = lax.axis_index("z")
    c = lax.axis_index("c")
    g = lax.axis_index("grp")
    at = jnp.stack([y, z, c, g]).astype(jnp.int32)
    other_kv = swap(prefix_kv)
    send, rows = pack_queries(prefix_id, place, queries)
    own_rows = [rows] + [turn(rows, k) for k in range(1, NY)]
    packed = pack_suffix(suffix_kv)
    arrived = lax.all_to_all(send, ("grp", "z"), 0, 0, tiled=True)
    arrived, packed = lax.optimization_barrier((arrived, packed))
    arrived = arrived.reshape(GRP, NZ, 32, HD)
    gathered = [arrived] + [turn(arrived, k) for k in range(1, NY)]
    suffix_own = lax.all_to_all(packed, ("z", "y"), 0, 0, tiled=True)
    suffix_other = swap(suffix_own)
    partials = prefix_attention(gathered, prefix_kv, other_kv)
    partials = suffix_attention(at, suffix_len, own_rows, suffix_own, suffix_other, new_kv, partials)
    parts = [partials[0]] + [turn(partials[k], -k) for k in range(1, NY)]
    back = lax.all_to_all(combine(parts), ("grp", "z"), 0, 0, tiled=True)
    return finish(at, prefix_id, place, back, parts)


def solution(mesh):
    inner = Mesh(mesh.devices.reshape(GRP, NZ, NY, NC), ("grp", "z", "y", "c"))
    ctx = ("z", "y", "c")
    return jax.shard_map(
        per_device,
        mesh=inner,
        in_specs=(
            P("grp", None, ctx),
            P("grp", ctx, None),
            P("grp", ctx, None),
            P("grp", None, None),
            P("grp", None),
            P(),
            P("grp"),
        ),
        out_specs=P("grp", None, ctx),
        check_vma=False,
    )
```

```python
import functools

import jax
import jax.numpy as jnp
from jax import lax
from jax.experimental import pallas as pl
from jax.experimental.pallas import tpu as pltpu
from jax.sharding import Mesh
from jax.sharding import PartitionSpec as P

GRP, NZ, NY, NC = 4, 8, 4, 2
HD = 128
STEPS = 4
REQ = 8
SPAN = 16
HALF = 1024
STATS = 32
ROWS = NZ * HD + STATS
TAIL = 32
MESSAGE = 4 * SPAN + 16
BACK = 40
ARRIVED = GRP * NZ * 32
CHUNK = 512
FACTOR = HD ** (-0.5) * 1.4426950408889634
NEG = -1e30
F32 = jnp.float32
BF16 = jnp.bfloat16


def nt_dot(a, b):
    return lax.dot_general(a, b, (((1,), (1,)), ((), ())), preferred_element_type=F32)


def tn_dot(a, b):
    return lax.dot_general(a, b, (((0,), (0,)), ((), ())), preferred_element_type=F32)


def slot_of(r, pid_ref, place_ref):
    chosen = [place_ref[pid_ref[i]] for i in range(r + 1)]
    rank = jnp.int32(0)
    for i in range(r):
        rank = rank + (chosen[i] == chosen[r]).astype(jnp.int32)
    return chosen[r] * 2 + rank


def pack_queries_kernel(pid_ref, place_ref, q_ref, send_ref, rows_ref, buf):
    buf[...] = jnp.zeros_like(buf)
    for pair in range(REQ // 2):
        both = []
        for r in (2 * pair, 2 * pair + 1):
            q = q_ref[r].astype(F32)
            rows = jnp.concatenate([q[:, :HD], q[:, HD:]], axis=0)
            buf[slot_of(r, pid_ref, place_ref)] = rows
            both.append(rows)
        rows_ref[pair] = jnp.concatenate(both, axis=0).astype(BF16)
    for g in range(GRP):
        block = buf[4 * g : 4 * g + 4].reshape(32, HD).astype(BF16)
        for z in range(NZ):
            send_ref[g * NZ + z] = block


def pack_queries(prefix_id, place, queries):
    return pl.pallas_call(
        pack_queries_kernel,
        out_shape=(
            jax.ShapeDtypeStruct((GRP * NZ, 32, HD), BF16),
            jax.ShapeDtypeStruct((REQ // 2, 16, HD), BF16),
        ),
        in_specs=[
            pl.BlockSpec(memory_space=pltpu.SMEM),
            pl.BlockSpec(memory_space=pltpu.SMEM),
            pl.BlockSpec(memory_space=pltpu.VMEM),
        ],
        out_specs=(
            pl.BlockSpec(memory_space=pltpu.VMEM),
            pl.BlockSpec(memory_space=pltpu.VMEM),
        ),
        scratch_shapes=[pltpu.VMEM((16, 8, HD), F32)],
        name="pack_queries",
    )(prefix_id, place, queries)


def pack_suffix_kernel(kv_ref, rows_ref, out_ref):
    for z in range(NZ):
        for y in range(NY):
            for r in range(2):
                for kind in range(2):
                    first = (2 * kind + r) * SPAN
                    block = kind * NZ + z
                    out_ref[z * NY + y, first : first + SPAN, :] = kv_ref[
                        2 * y + r, :, block * HD : (block + 1) * HD
                    ]
            out_ref[z * NY + y, 4 * SPAN :, :] = rows_ref[y]


def pack_suffix(suffix_kv, rows):
    return pl.pallas_call(
        pack_suffix_kernel,
        out_shape=jax.ShapeDtypeStruct((NZ * NY, MESSAGE, HD), BF16),
        in_specs=[pl.BlockSpec(memory_space=pltpu.VMEM)] * 2,
        out_specs=pl.BlockSpec(memory_space=pltpu.VMEM),
        name="pack_suffix",
    )(suffix_kv, rows)


def split_total(total):
    high = total.astype(BF16).astype(F32)
    return high, total - high


def lanes(block):
    return pl.ds(pl.multiple_of(block * HD, HD), HD)


def prefix_scores(queries, halves, z, p, score, peak):
    first = [pl.multiple_of((g * NZ + z) * 32 + p * 16, 16) for g in range(GRP)]
    q = jnp.concatenate([ref[pl.ds(row, 16), :] for ref in queries for row in first], axis=0)
    top = None
    for i, kv in enumerate(halves):
        for start in range(0, HALF, CHUNK):
            s = nt_dot(kv[p, start : start + CHUNK, lanes(z)], q)
            score[i * HALF + start : i * HALF + start + CHUNK, :] = s
            high = jnp.max(s.reshape(CHUNK // 8, 8, 256), axis=0)
            top = high if top is None else jnp.maximum(top, high)
    peak[...] = top


def prefix_values(halves, z, p, score, peak):
    top = jnp.max(peak[...], axis=0, keepdims=True) * FACTOR
    top = top.astype(BF16).astype(F32)
    total = jnp.zeros((8, 256), F32)
    summed = jnp.zeros((HD, 256), F32)
    for i, kv in enumerate(halves):
        for start in range(0, HALF, CHUNK):
            s = score[i * HALF + start : i * HALF + start + CHUNK, :]
            w = jnp.exp2(s * FACTOR - top)
            total = total + jnp.sum(w.reshape(CHUNK // 8, 8, 256), axis=0)
            v = kv[p, start : start + CHUNK, lanes(NZ + z)]
            summed = summed + tn_dot(v, w.astype(BF16))
    high, low = split_total(jnp.sum(total, axis=0, keepdims=True))
    return summed, (top, high, low)


def prefix_kernel(q0, q1, q2, q3, own, other, o0, o1, o2, o3, kv0, kv1, sa, sb, ma, mb, stats, sems):
    queries, halves = (q0, q1, q2, q3), (kv0, kv1)

    def fetch(half, kind, z):
        cols = lanes(kind * NZ + z)
        return pltpu.make_async_copy(
            (own, other)[half].at[:, :, cols], halves[half].at[:, :, cols], sems.at[half, kind, z]
        )

    for z in range(NZ):
        for kind in range(2):
            for half in range(2):
                fetch(half, kind, z).start()

    def ready(kind, z):
        fetch(0, kind, z).wait()
        fetch(1, kind, z).wait()

    def step(z, last):
        prefix_scores(queries, halves, z, 1, sb, mb)
        even = prefix_values(halves, z, 0, sa, ma)
        if not last:
            prefix_scores(queries, halves, z + 1, 0, sa, ma)
        odd = prefix_values(halves, z, 1, sb, mb)
        rows = pl.ds(pl.multiple_of(z * HD, HD), HD)
        for k, out in enumerate((o0, o1, o2, o3)):
            cols = slice(64 * k, 64 * (k + 1))
            out[rows, :] = jnp.concatenate([even[0][:, cols], odd[0][:, cols]], axis=1).astype(BF16)
            for i in range(3):
                stats[k, pl.ds(8 * i + z, 1), :] = jnp.concatenate(
                    [even[1][i][:, cols], odd[1][i][:, cols]], axis=1
                )

    stats[...] = jnp.zeros_like(stats)
    ready(0, 0)
    prefix_scores(queries, halves, 0, 0, sa, ma)

    def body(z, carry):
        ready(1, z)
        ready(0, z + 1)
        step(z, False)
        return carry

    lax.fori_loop(0, NZ - 1, body, 0)
    ready(1, NZ - 1)
    step(NZ - 1, True)
    for k, out in enumerate((o0, o1, o2, o3)):
        out[NZ * HD :, :] = stats[k].astype(BF16)


def prefix_attention(gathered, own, other):
    vmem = pl.BlockSpec(memory_space=pltpu.VMEM)
    hbm = pl.BlockSpec(memory_space=pl.ANY)
    return pl.pallas_call(
        prefix_kernel,
        out_shape=(jax.ShapeDtypeStruct((ROWS, HD), BF16),) * NY,
        in_specs=[vmem] * 4 + [hbm] * 2,
        out_specs=(vmem,) * NY,
        scratch_shapes=[
            pltpu.VMEM(own.shape, BF16),
            pltpu.VMEM(own.shape, BF16),
            pltpu.VMEM((2 * HALF, 256), F32),
            pltpu.VMEM((2 * HALF, 256), F32),
            pltpu.VMEM((8, 256), F32),
            pltpu.VMEM((8, 256), F32),
            pltpu.VMEM((NY, STATS, HD), F32),
            pltpu.SemaphoreType.DMA((2, 2, NZ)),
        ],
        compiler_params=pltpu.CompilerParams(vmem_limit_bytes=44 * 1024 * 1024),
        cost_estimate=pl.CostEstimate(
            flops=20 * 4096 * 2048 * HD, bytes_accessed=18 << 20, transcendentals=4096 * 2048
        ),
        name="prefix_attention",
    )(*gathered, own, other)


def suffix_kernel(len_ref, kv_own, kv_other, new_kv, o0, o1, o2, o3):
    y, z, core = lax.axis_index("y"), lax.axis_index("z"), lax.axis_index("c")
    index = lax.broadcasted_iota(jnp.int32, (32, 512), 1)
    base = (index // SPAN) * (2 * SPAN) + index % SPAN
    step = lax.broadcasted_iota(jnp.int32, (32, 1), 0) % STEPS
    sums, tops, totals = [], [], []
    queries = [
        kv_own[z * NY + lax.rem(y + NY - k, NY)].astype(F32)[4 * SPAN :] for k in range(NY)
    ]
    for r in range(2):
        length = len_ref[2 * y + r]
        keys, values = slice(r * SPAN, (r + 1) * SPAN), slice((2 + r) * SPAN, (3 + r) * SPAN)
        qf = jnp.concatenate([q[8 * r : 8 * r + 8] for q in queries], axis=0)
        q = qf.astype(BF16)
        scores = []
        for ref, c in ((kv_own, core), (kv_other, 1 - core)):
            s = nt_dot(q, ref[:, keys, :].reshape(512, HD)) * FACTOR
            scores.append(jnp.where(base + c * SPAN < length, s, NEG))
        kn = new_kv[2 * y + r, :, lanes(z)].astype(F32)
        vn = new_kv[2 * y + r, :, lanes(NZ + z)].astype(F32)
        fresh = []
        for t in range(STEPS):
            s = jnp.sum(qf * kn[t : t + 1], axis=1, keepdims=True) * FACTOR
            fresh.append(jnp.where(step >= t, s, NEG))
        top = functools.reduce(
            jnp.maximum, [jnp.max(s, axis=1, keepdims=True) for s in scores] + fresh
        )
        top = top.astype(BF16).astype(F32)
        total = jnp.zeros((32, 1), F32)
        summed = jnp.zeros((32, HD), F32)
        for s, ref in zip(scores, (kv_own, kv_other)):
            w = jnp.exp2(s - top)
            total = total + jnp.sum(w, axis=1, keepdims=True)
            summed = summed + jnp.dot(
                w.astype(BF16), ref[:, values, :].reshape(512, HD), preferred_element_type=F32
            )
        for t in range(STEPS):
            w = jnp.exp2(fresh[t] - top)
            total = total + w
            summed = summed + w.astype(BF16).astype(F32) * vn[t : t + 1]
        sums.append(summed)
        tops.append(top)
        totals.append(total)
    lane = lax.broadcasted_iota(jnp.int32, (16, HD), 1)
    for k, out in enumerate((o0, o1, o2, o3)):
        rows = slice(8 * k, 8 * k + 8)
        top = jnp.concatenate([t[rows] for t in tops], axis=0)
        high, low = split_total(jnp.concatenate([t[rows] for t in totals], axis=0))
        out[:16, :] = jnp.concatenate([s[rows] for s in sums], axis=0).astype(BF16)
        stat = jnp.where(
            lane == 0, top, jnp.where(lane == 1, high, jnp.where(lane == 2, low, 0.0))
        )
        out[16:, :] = stat.astype(BF16)


def suffix_attention(lengths, kv_own, kv_other, new_kv):
    vmem = pl.BlockSpec(memory_space=pltpu.VMEM)
    return pl.pallas_call(
        suffix_kernel,
        in_specs=[pl.BlockSpec(memory_space=pltpu.SMEM)] + [vmem] * 3,
        out_specs=[vmem] * NY,
        out_shape=[jax.ShapeDtypeStruct((TAIL, HD), BF16)] * NY,
        name="suffix_attention",
    )(lengths, kv_own, kv_other, new_kv)


def combine_kernel(p0, p1, p2, p3, out_ref):
    stats = [ref[NZ * HD :, :].astype(F32) for ref in (p0, p1, p2, p3)]
    top = functools.reduce(jnp.maximum, [s[:NZ] for s in stats])
    factors = [jnp.exp2(s[:NZ] - top) for s in stats]
    total = sum((s[NZ : 2 * NZ] + s[2 * NZ : 3 * NZ]) * f for s, f in zip(stats, factors))
    high, low = split_total(total)
    row = lax.broadcasted_iota(jnp.int32, (8, HD), 0)
    for z in range(NZ):
        at = slice(z, z + 1)
        rows = slice(z * HD, (z + 1) * HD)
        summed = sum(ref[rows].astype(F32) * f[at] for ref, f in zip((p0, p1, p2, p3), factors))
        stat = jnp.where(
            row == 0, top[at], jnp.where(row == 1, high[at], jnp.where(row == 2, low[at], 0.0))
        )
        turned = jnp.transpose(summed)
        for g in range(GRP):
            out_ref[g * NZ + z] = jnp.concatenate(
                [turned[16 * g : 16 * g + 16], turned[64 + 16 * g : 80 + 16 * g], stat], axis=0
            ).astype(BF16)


def combine(parts):
    spec = pl.BlockSpec(memory_space=pltpu.VMEM)
    return pl.pallas_call(
        combine_kernel,
        out_shape=jax.ShapeDtypeStruct((GRP * NZ, BACK, HD), BF16),
        in_specs=[spec] * 4,
        out_specs=spec,
        name="combine",
    )(*parts)


def finish_kernel(pid_ref, place_ref, back_ref, t0, t1, t2, t3, out_ref, turned, sums, tops, totals, tails):
    y, g = lax.axis_index("y"), lax.axis_index("grp")
    for k, ref in enumerate((t0, t1, t2, t3)):
        tails[k] = ref[...].astype(F32)
    blocks = [back_ref[s].astype(F32) for s in range(GRP * NZ)]
    rows = []
    for src in range(GRP):
        stats = [b[32:BACK] for b in blocks[src * NZ : (src + 1) * NZ]]
        top = functools.reduce(jnp.maximum, [s[0:1] for s in stats])
        factors = [jnp.exp2(s[0:1] - top) for s in stats]
        total = sum((s[1:2] + s[2:3]) * f for s, f in zip(stats, factors))
        rows += factors + [top, total, jnp.zeros((6, HD), F32)]
    rows.append(jnp.zeros((64, HD), F32))
    turned[...] = jnp.transpose(jnp.concatenate(rows, axis=0))
    cols = jnp.concatenate(
        [
            turned[pl.ds(pl.multiple_of(16 * g, 16), 16), :],
            turned[pl.ds(pl.multiple_of(64 + 16 * g, 16), 16), :],
        ],
        axis=0,
    )
    for src in range(GRP):
        col = [cols[:, 16 * src + i : 16 * src + i + 1] for i in range(10)]
        summed = sum(blocks[src * NZ + z][:32] * col[z] for z in range(NZ))
        sums[4 * src : 4 * src + 4] = summed.reshape(4, 8, HD)
        tops[4 * src : 4 * src + 4] = jnp.broadcast_to(col[8], (32, HD)).reshape(4, 8, HD)
        totals[4 * src : 4 * src + 4] = jnp.broadcast_to(col[9], (32, HD)).reshape(4, 8, HD)
    for r in range(REQ):
        slot = slot_of(r, pid_ref, place_ref)
        k = (r // 2 + NY - y) % NY
        tail = tails[k]
        base = 8 * (r % 2)
        s_sum = tail[base : base + 8]
        stat = tail[16 + base : 24 + base]
        s_top, s_total = stat[:, 0:1], stat[:, 1:2] + stat[:, 2:3]
        p_sum, p_top, p_total = sums[slot], tops[slot], totals[slot]
        top = jnp.maximum(p_top, s_top)
        left, right = jnp.exp2(p_top - top), jnp.exp2(s_top - top)
        result = (p_sum * left + s_sum * right) / (p_total * left + s_total * right)
        out_ref[r] = jnp.concatenate([result[:STEPS], result[STEPS:]], axis=1).astype(BF16)


def finish(prefix_id, place, back, tails):
    smem, vmem = (pl.BlockSpec(memory_space=space) for space in (pltpu.SMEM, pltpu.VMEM))
    return pl.pallas_call(
        finish_kernel,
        out_shape=jax.ShapeDtypeStruct((REQ, STEPS, 2 * HD), BF16),
        in_specs=[smem, smem] + [vmem] * 5,
        out_specs=vmem,
        scratch_shapes=[
            pltpu.VMEM((HD, HD), F32),
            pltpu.VMEM((16, 8, HD), F32),
            pltpu.VMEM((16, 8, HD), F32),
            pltpu.VMEM((16, 8, HD), F32),
            pltpu.VMEM((NY, TAIL, HD), F32),
        ],
        name="finish",
    )(prefix_id, place, back, *tails)


def turn(x, by):
    return lax.ppermute(x, "y", [(i, (i + by) % NY) for i in range(NY)])


def swap(x):
    return lax.ppermute(x, "c", [(0, 1), (1, 0)])


def per_device(queries, prefix_kv, suffix_kv, new_kv, prefix_id, place, suffix_len):
    other_kv = swap(prefix_kv)
    prefix_id = prefix_id.reshape(REQ)
    send, rows = pack_queries(prefix_id, place, queries)
    packed = pack_suffix(suffix_kv, rows)
    arrived = lax.all_to_all(send, ("grp", "z"), 0, 0, tiled=True)
    arrived, other_kv = lax.optimization_barrier((arrived, other_kv))
    arrived = arrived.reshape(ARRIVED, HD)
    gathered = [arrived] + [turn(arrived, k) for k in range(1, NY)]
    suffix_own = lax.all_to_all(packed, ("z", "y"), 0, 0, tiled=True)
    partials = list(prefix_attention(gathered, prefix_kv, other_kv))
    suffix_own, partials[0] = lax.optimization_barrier((suffix_own, partials[0]))
    parts = [partials[0]] + [turn(partials[k], -k) for k in range(1, NY)]
    suffix_other = swap(suffix_own)
    tails = suffix_attention(suffix_len, suffix_own, suffix_other, new_kv)
    tails = [tails[0]] + [turn(tails[k], -k) for k in range(1, NY)]
    joined = combine(parts)
    back = lax.all_to_all(joined, ("grp", "z"), 0, 0, tiled=True)
    return finish(prefix_id, place, back, tails)


def solution(mesh):
    inner = Mesh(mesh.devices.reshape(GRP, NZ, NY, NC), ("grp", "z", "y", "c"))
    ctx = ("z", "y", "c")
    return jax.shard_map(
        per_device,
        mesh=inner,
        in_specs=(
            P("grp", None, ctx),
            P("grp", ctx, None),
            P("grp", ctx, None),
            P("grp", None, None),
            P("grp", None),
            P(),
            P("grp"),
        ),
        out_specs=P("grp", None, ctx),
        check_vma=False,
    )
```

```python
import functools

import jax
import jax.numpy as jnp
from jax import lax
from jax.experimental import pallas as pl
from jax.experimental.pallas import tpu as pltpu
from jax.sharding import Mesh
from jax.sharding import PartitionSpec as P

GRP, NZ, NY, NC = 4, 8, 4, 2
HD = 128
STEPS = 4
REQ = 8
SPAN = 16
HALF = 1024
STATS = 32
ROWS = NZ * HD + STATS
TAIL = 32
MESSAGE = 4 * SPAN + 16
BACK = 40
ARRIVED = GRP * NZ * 32
CHUNK = 512
FACTOR = HD ** (-0.5) * 1.4426950408889634
NEG = -1e30
SMALL = 8 * 1024 * 1024
F32 = jnp.float32
BF16 = jnp.bfloat16


def nt_dot(a, b):
    return lax.dot_general(a, b, (((1,), (1,)), ((), ())), preferred_element_type=F32)


def tn_dot(a, b):
    return lax.dot_general(a, b, (((0,), (0,)), ((), ())), preferred_element_type=F32)


def slot_of(r, pid_ref, place_ref):
    chosen = [place_ref[pid_ref[i]] for i in range(r + 1)]
    rank = jnp.int32(0)
    for i in range(r):
        rank = rank + (chosen[i] == chosen[r]).astype(jnp.int32)
    return chosen[r] * 2 + rank


def pack_queries_kernel(pid_ref, place_ref, q_ref, send_ref, rows_ref, buf):
    buf[...] = jnp.zeros_like(buf)
    for pair in range(REQ // 2):
        both = []
        for r in (2 * pair, 2 * pair + 1):
            q = q_ref[r].astype(F32)
            rows = jnp.concatenate([q[:, :HD], q[:, HD:]], axis=0)
            buf[slot_of(r, pid_ref, place_ref)] = rows
            both.append(rows)
        rows_ref[pair] = jnp.concatenate(both, axis=0).astype(BF16)
    for g in range(GRP):
        block = buf[4 * g : 4 * g + 4].reshape(32, HD).astype(BF16)
        for z in range(NZ):
            send_ref[g * NZ + z] = block


def pack_queries(prefix_id, place, queries):
    return pl.pallas_call(
        pack_queries_kernel,
        out_shape=(
            jax.ShapeDtypeStruct((GRP * NZ, 32, HD), BF16),
            jax.ShapeDtypeStruct((REQ // 2, 16, HD), BF16),
        ),
        in_specs=[
            pl.BlockSpec(memory_space=pltpu.SMEM),
            pl.BlockSpec(memory_space=pltpu.SMEM),
            pl.BlockSpec(memory_space=pltpu.VMEM),
        ],
        out_specs=(
            pl.BlockSpec(memory_space=pltpu.VMEM),
            pl.BlockSpec(memory_space=pltpu.VMEM),
        ),
        scratch_shapes=[pltpu.VMEM((16, 8, HD), F32)],
        compiler_params=pltpu.CompilerParams(vmem_limit_bytes=SMALL),
        name="pack_queries",
    )(prefix_id, place, queries)


def pack_suffix_kernel(kv_ref, rows_ref, out_ref):
    for z in range(NZ):
        for y in range(NY):
            for r in range(2):
                for kind in range(2):
                    first = (2 * kind + r) * SPAN
                    block = kind * NZ + z
                    out_ref[z * NY + y, first : first + SPAN, :] = kv_ref[
                        2 * y + r, :, block * HD : (block + 1) * HD
                    ]
            out_ref[z * NY + y, 4 * SPAN :, :] = rows_ref[y]


def pack_suffix(suffix_kv, rows):
    return pl.pallas_call(
        pack_suffix_kernel,
        out_shape=jax.ShapeDtypeStruct((NZ * NY, MESSAGE, HD), BF16),
        in_specs=[pl.BlockSpec(memory_space=pltpu.VMEM)] * 2,
        out_specs=pl.BlockSpec(memory_space=pltpu.VMEM),
        compiler_params=pltpu.CompilerParams(vmem_limit_bytes=SMALL),
        name="pack_suffix",
    )(suffix_kv, rows)


def split_total(total):
    high = total.astype(BF16).astype(F32)
    return high, total - high


def lanes(block):
    return pl.ds(pl.multiple_of(block * HD, HD), HD)


def prefix_scores(queries, halves, z, p, score, peak):
    first = [pl.multiple_of((g * NZ + z) * 32 + p * 16, 16) for g in range(GRP)]
    q = jnp.concatenate([ref[pl.ds(row, 16), :] for ref in queries for row in first], axis=0)
    top = None
    for i, kv in enumerate(halves):
        for start in range(0, HALF, CHUNK):
            s = nt_dot(kv[p, start : start + CHUNK, lanes(z)], q)
            score[i * HALF + start : i * HALF + start + CHUNK, :] = s
            high = jnp.max(s.reshape(CHUNK // 8, 8, 256), axis=0)
            top = high if top is None else jnp.maximum(top, high)
    peak[...] = top


def prefix_values(halves, z, p, score, peak):
    top = jnp.max(peak[...], axis=0, keepdims=True) * FACTOR
    top = top.astype(BF16).astype(F32)
    total = jnp.zeros((8, 256), F32)
    summed = jnp.zeros((HD, 256), F32)
    for i, kv in enumerate(halves):
        for start in range(0, HALF, CHUNK):
            s = score[i * HALF + start : i * HALF + start + CHUNK, :]
            w = jnp.exp2(s * FACTOR - top)
            total = total + jnp.sum(w.reshape(CHUNK // 8, 8, 256), axis=0)
            v = kv[p, start : start + CHUNK, lanes(NZ + z)]
            summed = summed + tn_dot(v, w.astype(BF16))
    high, low = split_total(jnp.sum(total, axis=0, keepdims=True))
    return summed, (top, high, low)


def prefix_kernel(q0, q1, q2, q3, own, other, o0, o1, o2, o3, kv0, kv1, sa, sb, ma, mb, stats, sems):
    queries, halves = (q0, q1, q2, q3), (kv0, kv1)

    def fetch(half, kind, z):
        cols = lanes(kind * NZ + z)
        return pltpu.make_async_copy(
            (own, other)[half].at[:, :, cols], halves[half].at[:, :, cols], sems.at[half, kind, z]
        )

    for z in range(NZ):
        for kind in range(2):
            for half in range(2):
                fetch(half, kind, z).start()

    def ready(kind, z):
        fetch(0, kind, z).wait()
        fetch(1, kind, z).wait()

    def step(z, last):
        prefix_scores(queries, halves, z, 1, sb, mb)
        even = prefix_values(halves, z, 0, sa, ma)
        if not last:
            prefix_scores(queries, halves, z + 1, 0, sa, ma)
        odd = prefix_values(halves, z, 1, sb, mb)
        rows = pl.ds(pl.multiple_of(z * HD, HD), HD)
        for k, out in enumerate((o0, o1, o2, o3)):
            cols = slice(64 * k, 64 * (k + 1))
            out[rows, :] = jnp.concatenate([even[0][:, cols], odd[0][:, cols]], axis=1).astype(BF16)
            for i in range(3):
                stats[k, pl.ds(8 * i + z, 1), :] = jnp.concatenate(
                    [even[1][i][:, cols], odd[1][i][:, cols]], axis=1
                )

    stats[...] = jnp.zeros_like(stats)
    ready(0, 0)
    prefix_scores(queries, halves, 0, 0, sa, ma)

    def body(z, carry):
        ready(1, z)
        ready(0, z + 1)
        step(z, False)
        return carry

    lax.fori_loop(0, NZ - 1, body, 0)
    ready(1, NZ - 1)
    step(NZ - 1, True)
    for k, out in enumerate((o0, o1, o2, o3)):
        out[NZ * HD :, :] = stats[k].astype(BF16)


def prefix_attention(gathered, own, other):
    vmem = pl.BlockSpec(memory_space=pltpu.VMEM)
    hbm = pl.BlockSpec(memory_space=pl.ANY)
    return pl.pallas_call(
        prefix_kernel,
        out_shape=(jax.ShapeDtypeStruct((ROWS, HD), BF16),) * NY,
        in_specs=[vmem] * 4 + [hbm] * 2,
        out_specs=(vmem,) * NY,
        scratch_shapes=[
            pltpu.VMEM(own.shape, BF16),
            pltpu.VMEM(own.shape, BF16),
            pltpu.VMEM((2 * HALF, 256), F32),
            pltpu.VMEM((2 * HALF, 256), F32),
            pltpu.VMEM((8, 256), F32),
            pltpu.VMEM((8, 256), F32),
            pltpu.VMEM((NY, STATS, HD), F32),
            pltpu.SemaphoreType.DMA((2, 2, NZ)),
        ],
        compiler_params=pltpu.CompilerParams(vmem_limit_bytes=44 * 1024 * 1024),
        cost_estimate=pl.CostEstimate(
            flops=20 * 4096 * 2048 * HD, bytes_accessed=18 << 20, transcendentals=4096 * 2048
        ),
        name="prefix_attention",
    )(*gathered, own, other)


def suffix_kernel(len_ref, kv_own, kv_other, new_kv, o0, o1, o2, o3):
    y, z, core = lax.axis_index("y"), lax.axis_index("z"), lax.axis_index("c")
    index = lax.broadcasted_iota(jnp.int32, (32, 512), 1)
    base = (index // SPAN) * (2 * SPAN) + index % SPAN
    step = lax.broadcasted_iota(jnp.int32, (32, 1), 0) % STEPS
    sums, tops, totals = [], [], []
    queries = [
        kv_own[z * NY + lax.rem(y + NY - k, NY)].astype(F32)[4 * SPAN :] for k in range(NY)
    ]
    for r in range(2):
        length = len_ref[2 * y + r]
        keys, values = slice(r * SPAN, (r + 1) * SPAN), slice((2 + r) * SPAN, (3 + r) * SPAN)
        qf = jnp.concatenate([q[8 * r : 8 * r + 8] for q in queries], axis=0)
        q = qf.astype(BF16)
        scores = []
        for ref, c in ((kv_own, core), (kv_other, 1 - core)):
            s = nt_dot(q, ref[:, keys, :].reshape(512, HD)) * FACTOR
            scores.append(jnp.where(base + c * SPAN < length, s, NEG))
        kn = new_kv[2 * y + r, :, lanes(z)].astype(F32)
        vn = new_kv[2 * y + r, :, lanes(NZ + z)].astype(F32)
        fresh = []
        for t in range(STEPS):
            s = jnp.sum(qf * kn[t : t + 1], axis=1, keepdims=True) * FACTOR
            fresh.append(jnp.where(step >= t, s, NEG))
        top = functools.reduce(
            jnp.maximum, [jnp.max(s, axis=1, keepdims=True) for s in scores] + fresh
        )
        top = top.astype(BF16).astype(F32)
        total = jnp.zeros((32, 1), F32)
        summed = jnp.zeros((32, HD), F32)
        for s, ref in zip(scores, (kv_own, kv_other)):
            w = jnp.exp2(s - top)
            total = total + jnp.sum(w, axis=1, keepdims=True)
            summed = summed + jnp.dot(
                w.astype(BF16), ref[:, values, :].reshape(512, HD), preferred_element_type=F32
            )
        for t in range(STEPS):
            w = jnp.exp2(fresh[t] - top)
            total = total + w
            summed = summed + w.astype(BF16).astype(F32) * vn[t : t + 1]
        sums.append(summed)
        tops.append(top)
        totals.append(total)
    lane = lax.broadcasted_iota(jnp.int32, (16, HD), 1)
    for k, out in enumerate((o0, o1, o2, o3)):
        rows = slice(8 * k, 8 * k + 8)
        top = jnp.concatenate([t[rows] for t in tops], axis=0)
        high, low = split_total(jnp.concatenate([t[rows] for t in totals], axis=0))
        out[:16, :] = jnp.concatenate([s[rows] for s in sums], axis=0).astype(BF16)
        stat = jnp.where(
            lane == 0, top, jnp.where(lane == 1, high, jnp.where(lane == 2, low, 0.0))
        )
        out[16:, :] = stat.astype(BF16)


def suffix_attention(lengths, kv_own, kv_other, new_kv):
    vmem = pl.BlockSpec(memory_space=pltpu.VMEM)
    return pl.pallas_call(
        suffix_kernel,
        in_specs=[pl.BlockSpec(memory_space=pltpu.SMEM)] + [vmem] * 3,
        out_specs=[vmem] * NY,
        out_shape=[jax.ShapeDtypeStruct((TAIL, HD), BF16)] * NY,
        cost_estimate=pl.CostEstimate(flops=1 << 20, bytes_accessed=1 << 16, transcendentals=0),
        compiler_params=pltpu.CompilerParams(vmem_limit_bytes=SMALL),
        name="suffix_attention",
    )(lengths, kv_own, kv_other, new_kv)


def combine_kernel(p0, p1, p2, p3, out_ref):
    stats = [ref[NZ * HD :, :].astype(F32) for ref in (p0, p1, p2, p3)]
    top = functools.reduce(jnp.maximum, [s[:NZ] for s in stats])
    factors = [jnp.exp2(s[:NZ] - top) for s in stats]
    total = sum((s[NZ : 2 * NZ] + s[2 * NZ : 3 * NZ]) * f for s, f in zip(stats, factors))
    high, low = split_total(total)
    row = lax.broadcasted_iota(jnp.int32, (8, HD), 0)
    for z in range(NZ):
        at = slice(z, z + 1)
        rows = slice(z * HD, (z + 1) * HD)
        summed = sum(ref[rows].astype(F32) * f[at] for ref, f in zip((p0, p1, p2, p3), factors))
        stat = jnp.where(
            row == 0, top[at], jnp.where(row == 1, high[at], jnp.where(row == 2, low[at], 0.0))
        )
        turned = jnp.transpose(summed)
        for g in range(GRP):
            out_ref[g * NZ + z] = jnp.concatenate(
                [turned[16 * g : 16 * g + 16], turned[64 + 16 * g : 80 + 16 * g], stat], axis=0
            ).astype(BF16)


def combine(parts):
    spec = pl.BlockSpec(memory_space=pltpu.VMEM)
    return pl.pallas_call(
        combine_kernel,
        out_shape=jax.ShapeDtypeStruct((GRP * NZ, BACK, HD), BF16),
        in_specs=[spec] * 4,
        out_specs=spec,
        compiler_params=pltpu.CompilerParams(vmem_limit_bytes=SMALL),
        name="combine",
    )(*parts)


def finish_kernel(pid_ref, place_ref, back_ref, t0, t1, t2, t3, out_ref, turned, sums, tops, totals, tails):
    y, g = lax.axis_index("y"), lax.axis_index("grp")
    for k, ref in enumerate((t0, t1, t2, t3)):
        tails[k] = ref[...].astype(F32)
    blocks = [back_ref[s].astype(F32) for s in range(GRP * NZ)]
    rows = []
    for src in range(GRP):
        stats = [b[32:BACK] for b in blocks[src * NZ : (src + 1) * NZ]]
        top = functools.reduce(jnp.maximum, [s[0:1] for s in stats])
        factors = [jnp.exp2(s[0:1] - top) for s in stats]
        total = sum((s[1:2] + s[2:3]) * f for s, f in zip(stats, factors))
        rows += factors + [top, total, jnp.zeros((6, HD), F32)]
    rows.append(jnp.zeros((64, HD), F32))
    turned[...] = jnp.transpose(jnp.concatenate(rows, axis=0))
    cols = jnp.concatenate(
        [
            turned[pl.ds(pl.multiple_of(16 * g, 16), 16), :],
            turned[pl.ds(pl.multiple_of(64 + 16 * g, 16), 16), :],
        ],
        axis=0,
    )
    for src in range(GRP):
        col = [cols[:, 16 * src + i : 16 * src + i + 1] for i in range(10)]
        summed = sum(blocks[src * NZ + z][:32] * col[z] for z in range(NZ))
        sums[4 * src : 4 * src + 4] = summed.reshape(4, 8, HD)
        tops[4 * src : 4 * src + 4] = jnp.broadcast_to(col[8], (32, HD)).reshape(4, 8, HD)
        totals[4 * src : 4 * src + 4] = jnp.broadcast_to(col[9], (32, HD)).reshape(4, 8, HD)
    for r in range(REQ):
        slot = slot_of(r, pid_ref, place_ref)
        k = (r // 2 + NY - y) % NY
        tail = tails[k]
        base = 8 * (r % 2)
        s_sum = tail[base : base + 8]
        stat = tail[16 + base : 24 + base]
        s_top, s_total = stat[:, 0:1], stat[:, 1:2] + stat[:, 2:3]
        p_sum, p_top, p_total = sums[slot], tops[slot], totals[slot]
        top = jnp.maximum(p_top, s_top)
        left, right = jnp.exp2(p_top - top), jnp.exp2(s_top - top)
        result = (p_sum * left + s_sum * right) / (p_total * left + s_total * right)
        out_ref[r] = jnp.concatenate([result[:STEPS], result[STEPS:]], axis=1).astype(BF16)


def finish(prefix_id, place, back, tails):
    smem, vmem = (pl.BlockSpec(memory_space=space) for space in (pltpu.SMEM, pltpu.VMEM))
    return pl.pallas_call(
        finish_kernel,
        out_shape=jax.ShapeDtypeStruct((REQ, STEPS, 2 * HD), BF16),
        in_specs=[smem, smem] + [vmem] * 5,
        out_specs=vmem,
        scratch_shapes=[
            pltpu.VMEM((HD, HD), F32),
            pltpu.VMEM((16, 8, HD), F32),
            pltpu.VMEM((16, 8, HD), F32),
            pltpu.VMEM((16, 8, HD), F32),
            pltpu.VMEM((NY, TAIL, HD), F32),
        ],
        compiler_params=pltpu.CompilerParams(vmem_limit_bytes=SMALL),
        name="finish",
    )(prefix_id, place, back, *tails)


def turn(x, by):
    return lax.ppermute(x, "y", [(i, (i + by) % NY) for i in range(NY)])


def swap(x):
    return lax.ppermute(x, "c", [(0, 1), (1, 0)])


def per_device(queries, prefix_kv, suffix_kv, new_kv, prefix_id, place, suffix_len):
    other_kv = swap(prefix_kv)
    prefix_id = prefix_id.reshape(REQ)
    send, rows = pack_queries(prefix_id, place, queries)
    packed = pack_suffix(suffix_kv, rows)
    arrived = lax.all_to_all(send, ("grp", "z"), 0, 0, tiled=True)
    arrived, other_kv = lax.optimization_barrier((arrived, other_kv))
    arrived = arrived.reshape(ARRIVED, HD)
    gathered = [arrived] + [turn(arrived, k) for k in range(1, NY)]
    suffix_own = lax.all_to_all(packed, ("z", "y"), 0, 0, tiled=True)
    partials = list(prefix_attention(gathered, prefix_kv, other_kv))
    suffix_own, partials[0] = lax.optimization_barrier((suffix_own, partials[0]))
    parts = [partials[0]] + [turn(partials[k], -k) for k in range(1, NY)]
    suffix_other = swap(suffix_own)
    tails = suffix_attention(suffix_len, suffix_own, suffix_other, new_kv)
    tails = [tails[0]] + [turn(tails[k], -k) for k in range(1, NY)]
    joined = combine(parts)
    back = lax.all_to_all(joined, ("grp", "z"), 0, 0, tiled=True)
    return finish(prefix_id, place, back, tails)


def solution(mesh):
    inner = Mesh(mesh.devices.reshape(GRP, NZ, NY, NC), ("grp", "z", "y", "c"))
    ctx = ("z", "y", "c")
    return jax.shard_map(
        per_device,
        mesh=inner,
        in_specs=(
            P("grp", None, ctx),
            P("grp", ctx, None),
            P("grp", ctx, None),
            P("grp", None, None),
            P("grp", None),
            P(),
            P("grp"),
        ),
        out_specs=P("grp", None, ctx),
        check_vma=False,
    )
```

```python
import functools

import jax
import jax.numpy as jnp
from jax import lax
from jax.experimental import pallas as pl
from jax.experimental.pallas import tpu as pltpu
from jax.sharding import Mesh
from jax.sharding import PartitionSpec as P

GRP, NZ, NY, NC = 4, 8, 4, 2
HD = 128
STEPS = 4
REQ = 8
SPAN = 16
HALF = 1024
STATS = 32
ROWS = NZ * HD + STATS
TAIL = 32
MESSAGE = 4 * SPAN + 16
BACK = 40
ARRIVED = GRP * NZ * 32
CHUNK = 512
FACTOR = HD ** (-0.5) * 1.4426950408889634
NEG = -1e30
SMALL = 8 * 1024 * 1024
F32 = jnp.float32
BF16 = jnp.bfloat16


def nt_dot(a, b):
    return lax.dot_general(a, b, (((1,), (1,)), ((), ())), preferred_element_type=F32)


def tn_dot(a, b):
    return lax.dot_general(a, b, (((0,), (0,)), ((), ())), preferred_element_type=F32)


def slot_of(r, pid_ref, place_ref):
    chosen = [place_ref[pid_ref[i]] for i in range(r + 1)]
    rank = jnp.int32(0)
    for i in range(r):
        rank = rank + (chosen[i] == chosen[r]).astype(jnp.int32)
    return chosen[r] * 2 + rank


def pack_queries_kernel(pid_ref, place_ref, q_ref, send_ref, rows_ref, buf):
    buf[...] = jnp.zeros_like(buf)
    for pair in range(REQ // 2):
        both = []
        for r in (2 * pair, 2 * pair + 1):
            q = q_ref[r].astype(F32)
            rows = jnp.concatenate([q[:, :HD], q[:, HD:]], axis=0)
            buf[slot_of(r, pid_ref, place_ref)] = rows
            both.append(rows)
        rows_ref[pair] = jnp.concatenate(both, axis=0).astype(BF16)
    for g in range(GRP):
        block = buf[4 * g : 4 * g + 4].reshape(32, HD).astype(BF16)
        for z in range(NZ):
            send_ref[z * GRP + g] = block


def pack_queries(prefix_id, place, queries):
    return pl.pallas_call(
        pack_queries_kernel,
        out_shape=(
            jax.ShapeDtypeStruct((GRP * NZ, 32, HD), BF16),
            jax.ShapeDtypeStruct((REQ // 2, 16, HD), BF16),
        ),
        in_specs=[
            pl.BlockSpec(memory_space=pltpu.SMEM),
            pl.BlockSpec(memory_space=pltpu.SMEM),
            pl.BlockSpec(memory_space=pltpu.VMEM),
        ],
        out_specs=(
            pl.BlockSpec(memory_space=pltpu.VMEM),
            pl.BlockSpec(memory_space=pltpu.VMEM),
        ),
        scratch_shapes=[pltpu.VMEM((16, 8, HD), F32)],
        name="pack_queries",
    )(prefix_id, place, queries)


def pack_suffix_kernel(kv_ref, rows_ref, out_ref):
    for z in range(NZ):
        for y in range(NY):
            for r in range(2):
                for kind in range(2):
                    first = (2 * kind + r) * SPAN
                    block = kind * NZ + z
                    out_ref[y * NZ + z, first : first + SPAN, :] = kv_ref[
                        2 * y + r, :, block * HD : (block + 1) * HD
                    ]
            out_ref[y * NZ + z, 4 * SPAN :, :] = rows_ref[y]


def pack_suffix(suffix_kv, rows):
    return pl.pallas_call(
        pack_suffix_kernel,
        out_shape=jax.ShapeDtypeStruct((NZ * NY, MESSAGE, HD), BF16),
        in_specs=[pl.BlockSpec(memory_space=pltpu.VMEM)] * 2,
        out_specs=pl.BlockSpec(memory_space=pltpu.VMEM),
        compiler_params=pltpu.CompilerParams(vmem_limit_bytes=SMALL),
        name="pack_suffix",
    )(suffix_kv, rows)


def split_total(total):
    high = total.astype(BF16).astype(F32)
    return high, total - high


def lanes(block):
    return pl.ds(pl.multiple_of(block * HD, HD), HD)


def prefix_scores(queries, halves, z, p, score, peak):
    first = [pl.multiple_of((z * GRP + g) * 32 + p * 16, 16) for g in range(GRP)]
    q = jnp.concatenate([ref[pl.ds(row, 16), :] for ref in queries for row in first], axis=0)
    top = None
    for i, kv in enumerate(halves):
        for start in range(0, HALF, CHUNK):
            s = nt_dot(kv[p, start : start + CHUNK, lanes(z)], q)
            score[i * HALF + start : i * HALF + start + CHUNK, :] = s
            high = jnp.max(s.reshape(CHUNK // 8, 8, 256), axis=0)
            top = high if top is None else jnp.maximum(top, high)
    peak[...] = top


def prefix_values(halves, z, p, score, peak):
    top = jnp.max(peak[...], axis=0, keepdims=True) * FACTOR
    top = top.astype(BF16).astype(F32)
    total = jnp.zeros((8, 256), F32)
    summed = jnp.zeros((HD, 256), F32)
    for i, kv in enumerate(halves):
        for start in range(0, HALF, CHUNK):
            s = score[i * HALF + start : i * HALF + start + CHUNK, :]
            w = jnp.exp2(s * FACTOR - top)
            total = total + jnp.sum(w.reshape(CHUNK // 8, 8, 256), axis=0)
            v = kv[p, start : start + CHUNK, lanes(NZ + z)]
            summed = summed + tn_dot(v, w.astype(BF16))
    high, low = split_total(jnp.sum(total, axis=0, keepdims=True))
    return summed, (top, high, low)


def prefix_kernel(q0, q1, q2, q3, own, other, o0, o1, o2, o3, kv0, kv1, sa, sb, ma, mb, stats, sems):
    queries, halves = (q0, q1, q2, q3), (kv0, kv1)

    def fetch(half, kind, z):
        cols = lanes(kind * NZ + z)
        return pltpu.make_async_copy(
            (own, other)[half].at[:, :, cols], halves[half].at[:, :, cols], sems.at[half, kind, z]
        )

    for z in range(NZ):
        for kind in range(2):
            for half in range(2):
                fetch(half, kind, z).start()

    def ready(kind, z):
        fetch(0, kind, z).wait()
        fetch(1, kind, z).wait()

    def step(z, last):
        prefix_scores(queries, halves, z, 1, sb, mb)
        even = prefix_values(halves, z, 0, sa, ma)
        if not last:
            prefix_scores(queries, halves, z + 1, 0, sa, ma)
        odd = prefix_values(halves, z, 1, sb, mb)
        rows = pl.ds(pl.multiple_of(z * HD, HD), HD)
        for k, out in enumerate((o0, o1, o2, o3)):
            cols = slice(64 * k, 64 * (k + 1))
            out[rows, :] = jnp.concatenate([even[0][:, cols], odd[0][:, cols]], axis=1).astype(BF16)
            for i in range(3):
                stats[k, pl.ds(8 * i + z, 1), :] = jnp.concatenate(
                    [even[1][i][:, cols], odd[1][i][:, cols]], axis=1
                )

    stats[...] = jnp.zeros_like(stats)
    ready(0, 0)
    prefix_scores(queries, halves, 0, 0, sa, ma)

    def body(z, carry):
        ready(1, z)
        ready(0, z + 1)
        step(z, False)
        return carry

    lax.fori_loop(0, NZ - 1, body, 0)
    ready(1, NZ - 1)
    step(NZ - 1, True)
    for k, out in enumerate((o0, o1, o2, o3)):
        out[NZ * HD :, :] = stats[k].astype(BF16)


def prefix_attention(gathered, own, other):
    vmem = pl.BlockSpec(memory_space=pltpu.VMEM)
    hbm = pl.BlockSpec(memory_space=pl.ANY)
    return pl.pallas_call(
        prefix_kernel,
        out_shape=(jax.ShapeDtypeStruct((ROWS, HD), BF16),) * NY,
        in_specs=[vmem] * 4 + [hbm] * 2,
        out_specs=(vmem,) * NY,
        scratch_shapes=[
            pltpu.VMEM(own.shape, BF16),
            pltpu.VMEM(own.shape, BF16),
            pltpu.VMEM((2 * HALF, 256), F32),
            pltpu.VMEM((2 * HALF, 256), F32),
            pltpu.VMEM((8, 256), F32),
            pltpu.VMEM((8, 256), F32),
            pltpu.VMEM((NY, STATS, HD), F32),
            pltpu.SemaphoreType.DMA((2, 2, NZ)),
        ],
        compiler_params=pltpu.CompilerParams(vmem_limit_bytes=44 * 1024 * 1024),
        cost_estimate=pl.CostEstimate(
            flops=20 * 4096 * 2048 * HD, bytes_accessed=18 << 20, transcendentals=4096 * 2048
        ),
        name="prefix_attention",
    )(*gathered, own, other)


def suffix_kernel(len_ref, kv_own, kv_other, new_kv, o0, o1, o2, o3):
    y, z, core = lax.axis_index("y"), lax.axis_index("z"), lax.axis_index("c")
    index = lax.broadcasted_iota(jnp.int32, (32, 512), 1)
    source = index // SPAN
    base = (source % NZ * NY + source // NZ) * (2 * SPAN) + index % SPAN
    step = lax.broadcasted_iota(jnp.int32, (32, 1), 0) % STEPS
    sums, tops, totals = [], [], []
    queries = [
        kv_own[lax.rem(y + NY - k, NY) * NZ + z].astype(F32)[4 * SPAN :] for k in range(NY)
    ]
    for r in range(2):
        length = len_ref[2 * y + r]
        keys, values = slice(r * SPAN, (r + 1) * SPAN), slice((2 + r) * SPAN, (3 + r) * SPAN)
        qf = jnp.concatenate([q[8 * r : 8 * r + 8] for q in queries], axis=0)
        q = qf.astype(BF16)
        scores = []
        for ref, c in ((kv_own, core), (kv_other, 1 - core)):
            s = nt_dot(q, ref[:, keys, :].reshape(512, HD)) * FACTOR
            scores.append(jnp.where(base + c * SPAN < length, s, NEG))
        kn = new_kv[2 * y + r, :, lanes(z)].astype(F32)
        vn = new_kv[2 * y + r, :, lanes(NZ + z)].astype(F32)
        fresh = []
        for t in range(STEPS):
            s = jnp.sum(qf * kn[t : t + 1], axis=1, keepdims=True) * FACTOR
            fresh.append(jnp.where(step >= t, s, NEG))
        top = functools.reduce(
            jnp.maximum, [jnp.max(s, axis=1, keepdims=True) for s in scores] + fresh
        )
        top = top.astype(BF16).astype(F32)
        total = jnp.zeros((32, 1), F32)
        summed = jnp.zeros((32, HD), F32)
        for s, ref in zip(scores, (kv_own, kv_other)):
            w = jnp.exp2(s - top)
            total = total + jnp.sum(w, axis=1, keepdims=True)
            summed = summed + jnp.dot(
                w.astype(BF16), ref[:, values, :].reshape(512, HD), preferred_element_type=F32
            )
        for t in range(STEPS):
            w = jnp.exp2(fresh[t] - top)
            total = total + w
            summed = summed + w.astype(BF16).astype(F32) * vn[t : t + 1]
        sums.append(summed)
        tops.append(top)
        totals.append(total)
    lane = lax.broadcasted_iota(jnp.int32, (16, HD), 1)
    for k, out in enumerate((o0, o1, o2, o3)):
        rows = slice(8 * k, 8 * k + 8)
        top = jnp.concatenate([t[rows] for t in tops], axis=0)
        high, low = split_total(jnp.concatenate([t[rows] for t in totals], axis=0))
        out[:16, :] = jnp.concatenate([s[rows] for s in sums], axis=0).astype(BF16)
        stat = jnp.where(
            lane == 0, top, jnp.where(lane == 1, high, jnp.where(lane == 2, low, 0.0))
        )
        out[16:, :] = stat.astype(BF16)


def suffix_attention(lengths, kv_own, kv_other, new_kv):
    vmem = pl.BlockSpec(memory_space=pltpu.VMEM)
    return pl.pallas_call(
        suffix_kernel,
        in_specs=[pl.BlockSpec(memory_space=pltpu.SMEM)] + [vmem] * 3,
        out_specs=[vmem] * NY,
        out_shape=[jax.ShapeDtypeStruct((TAIL, HD), BF16)] * NY,
        cost_estimate=pl.CostEstimate(flops=1 << 20, bytes_accessed=1 << 16, transcendentals=0),
        compiler_params=pltpu.CompilerParams(vmem_limit_bytes=SMALL),
        name="suffix_attention",
    )(lengths, kv_own, kv_other, new_kv)


def combine_kernel(p0, p1, p2, p3, out_ref):
    stats = [ref[NZ * HD :, :].astype(F32) for ref in (p0, p1, p2, p3)]
    top = functools.reduce(jnp.maximum, [s[:NZ] for s in stats])
    factors = [jnp.exp2(s[:NZ] - top) for s in stats]
    total = sum((s[NZ : 2 * NZ] + s[2 * NZ : 3 * NZ]) * f for s, f in zip(stats, factors))
    high, low = split_total(total)
    row = lax.broadcasted_iota(jnp.int32, (8, HD), 0)
    for z in range(NZ):
        at = slice(z, z + 1)
        rows = slice(z * HD, (z + 1) * HD)
        summed = sum(ref[rows].astype(F32) * f[at] for ref, f in zip((p0, p1, p2, p3), factors))
        stat = jnp.where(
            row == 0, top[at], jnp.where(row == 1, high[at], jnp.where(row == 2, low[at], 0.0))
        )
        turned = jnp.transpose(summed)
        for g in range(GRP):
            out_ref[z * GRP + g] = jnp.concatenate(
                [turned[16 * g : 16 * g + 16], turned[64 + 16 * g : 80 + 16 * g], stat], axis=0
            ).astype(BF16)


def combine(parts):
    spec = pl.BlockSpec(memory_space=pltpu.VMEM)
    return pl.pallas_call(
        combine_kernel,
        out_shape=jax.ShapeDtypeStruct((GRP * NZ, BACK, HD), BF16),
        in_specs=[spec] * 4,
        out_specs=spec,
        compiler_params=pltpu.CompilerParams(vmem_limit_bytes=SMALL),
        name="combine",
    )(*parts)


def finish_kernel(pid_ref, place_ref, back_ref, t0, t1, t2, t3, out_ref, turned, sums, tops, totals, tails):
    y, g = lax.axis_index("y"), lax.axis_index("grp")
    for k, ref in enumerate((t0, t1, t2, t3)):
        tails[k] = ref[...].astype(F32)
    blocks = [back_ref[s].astype(F32) for s in range(GRP * NZ)]
    rows = []
    for src in range(GRP):
        stats = [b[32:BACK] for b in blocks[src::GRP]]
        top = functools.reduce(jnp.maximum, [s[0:1] for s in stats])
        factors = [jnp.exp2(s[0:1] - top) for s in stats]
        total = sum((s[1:2] + s[2:3]) * f for s, f in zip(stats, factors))
        rows += factors + [top, total, jnp.zeros((6, HD), F32)]
    rows.append(jnp.zeros((64, HD), F32))
    turned[...] = jnp.transpose(jnp.concatenate(rows, axis=0))
    cols = jnp.concatenate(
        [
            turned[pl.ds(pl.multiple_of(16 * g, 16), 16), :],
            turned[pl.ds(pl.multiple_of(64 + 16 * g, 16), 16), :],
        ],
        axis=0,
    )
    for src in range(GRP):
        col = [cols[:, 16 * src + i : 16 * src + i + 1] for i in range(10)]
        summed = sum(blocks[z * GRP + src][:32] * col[z] for z in range(NZ))
        sums[4 * src : 4 * src + 4] = summed.reshape(4, 8, HD)
        tops[4 * src : 4 * src + 4] = jnp.broadcast_to(col[8], (32, HD)).reshape(4, 8, HD)
        totals[4 * src : 4 * src + 4] = jnp.broadcast_to(col[9], (32, HD)).reshape(4, 8, HD)
    for r in range(REQ):
        slot = slot_of(r, pid_ref, place_ref)
        k = (r // 2 + NY - y) % NY
        tail = tails[k]
        base = 8 * (r % 2)
        s_sum = tail[base : base + 8]
        stat = tail[16 + base : 24 + base]
        s_top, s_total = stat[:, 0:1], stat[:, 1:2] + stat[:, 2:3]
        p_sum, p_top, p_total = sums[slot], tops[slot], totals[slot]
        top = jnp.maximum(p_top, s_top)
        left, right = jnp.exp2(p_top - top), jnp.exp2(s_top - top)
        result = (p_sum * left + s_sum * right) / (p_total * left + s_total * right)
        out_ref[r] = jnp.concatenate([result[:STEPS], result[STEPS:]], axis=1).astype(BF16)


def finish(prefix_id, place, back, tails):
    smem, vmem = (pl.BlockSpec(memory_space=space) for space in (pltpu.SMEM, pltpu.VMEM))
    return pl.pallas_call(
        finish_kernel,
        out_shape=jax.ShapeDtypeStruct((REQ, STEPS, 2 * HD), BF16),
        in_specs=[smem, smem] + [vmem] * 5,
        out_specs=vmem,
        scratch_shapes=[
            pltpu.VMEM((HD, HD), F32),
            pltpu.VMEM((16, 8, HD), F32),
            pltpu.VMEM((16, 8, HD), F32),
            pltpu.VMEM((16, 8, HD), F32),
            pltpu.VMEM((NY, TAIL, HD), F32),
        ],
        compiler_params=pltpu.CompilerParams(vmem_limit_bytes=SMALL),
        name="finish",
    )(prefix_id, place, back, *tails)


def turn(x, by):
    return lax.ppermute(x, "y", [(i, (i + by) % NY) for i in range(NY)])


def swap(x):
    return lax.ppermute(x, "c", [(0, 1), (1, 0)])


def per_device(queries, prefix_kv, suffix_kv, new_kv, prefix_id, place, suffix_len):
    other_kv = swap(prefix_kv)
    prefix_id = prefix_id.reshape(REQ)
    send, rows = pack_queries(prefix_id, place, queries)
    packed = pack_suffix(suffix_kv, rows)
    arrived = lax.all_to_all(send, ("z", "grp"), 0, 0, tiled=True)
    arrived, other_kv = lax.optimization_barrier((arrived, other_kv))
    arrived = arrived.reshape(ARRIVED, HD)
    gathered = [arrived] + [turn(arrived, k) for k in range(1, NY)]
    suffix_own = lax.all_to_all(packed, ("y", "z"), 0, 0, tiled=True)
    partials = list(prefix_attention(gathered, prefix_kv, other_kv))
    suffix_own, partials[0] = lax.optimization_barrier((suffix_own, partials[0]))
    parts = [partials[0]] + [turn(partials[k], -k) for k in range(1, NY)]
    suffix_other = swap(suffix_own)
    tails = suffix_attention(suffix_len, suffix_own, suffix_other, new_kv)
    tails = [tails[0]] + [turn(tails[k], -k) for k in range(1, NY)]
    joined = combine(parts)
    back = lax.all_to_all(joined, ("z", "grp"), 0, 0, tiled=True)
    return finish(prefix_id, place, back, tails)


def solution(mesh):
    inner = Mesh(mesh.devices.reshape(GRP, NZ, NY, NC), ("grp", "z", "y", "c"))
    ctx = ("z", "y", "c")
    return jax.shard_map(
        per_device,
        mesh=inner,
        in_specs=(
            P("grp", None, ctx),
            P("grp", ctx, None),
            P("grp", ctx, None),
            P("grp", None, None),
            P("grp", None),
            P(),
            P("grp"),
        ),
        out_specs=P("grp", None, ctx),
        check_vma=False,
    )
```

```python
import functools

import jax
import jax.numpy as jnp
from jax import lax
from jax.experimental import pallas as pl
from jax.experimental.pallas import tpu as pltpu
from jax.sharding import Mesh
from jax.sharding import PartitionSpec as P

GRP, NZ, NY, NC = 4, 8, 4, 2
HD = 128
STEPS = 4
REQ = 8
SPAN = 16
HALF = 1024
STATS = 16
ROWS = NZ * HD + STATS
TAIL = 32
MESSAGE = 4 * SPAN + 16
BACK = 40
ARRIVED = GRP * NZ * 32
CHUNK = 512
FACTOR = HD ** (-0.5) * 1.4426950408889634
NEG = -1e30
SMALL = 8 * 1024 * 1024
F32 = jnp.float32
BF16 = jnp.bfloat16


def nt_dot(a, b):
    return lax.dot_general(a, b, (((1,), (1,)), ((), ())), preferred_element_type=F32)


def tn_dot(a, b):
    return lax.dot_general(a, b, (((0,), (0,)), ((), ())), preferred_element_type=F32)


def slot_of(r, pid_ref, place_ref):
    chosen = [place_ref[pid_ref[i]] for i in range(r + 1)]
    rank = jnp.int32(0)
    for i in range(r):
        rank = rank + (chosen[i] == chosen[r]).astype(jnp.int32)
    return chosen[r] * 2 + rank


def pack_queries_kernel(pid_ref, place_ref, q_ref, send_ref, rows_ref, buf):
    buf[...] = jnp.zeros_like(buf)
    for pair in range(REQ // 2):
        both = []
        for r in (2 * pair, 2 * pair + 1):
            q = q_ref[r].astype(F32)
            rows = jnp.concatenate([q[:, :HD], q[:, HD:]], axis=0)
            buf[slot_of(r, pid_ref, place_ref)] = rows
            both.append(rows)
        rows_ref[pair] = jnp.concatenate(both, axis=0).astype(BF16)
    for g in range(GRP):
        block = buf[4 * g : 4 * g + 4].reshape(32, HD).astype(BF16)
        for z in range(NZ):
            send_ref[z * GRP + g] = block


def pack_queries(prefix_id, place, queries):
    return pl.pallas_call(
        pack_queries_kernel,
        out_shape=(
            jax.ShapeDtypeStruct((GRP * NZ, 32, HD), BF16),
            jax.ShapeDtypeStruct((REQ // 2, 16, HD), BF16),
        ),
        in_specs=[
            pl.BlockSpec(memory_space=pltpu.SMEM),
            pl.BlockSpec(memory_space=pltpu.SMEM),
            pl.BlockSpec(memory_space=pltpu.VMEM),
        ],
        out_specs=(
            pl.BlockSpec(memory_space=pltpu.VMEM),
            pl.BlockSpec(memory_space=pltpu.VMEM),
        ),
        scratch_shapes=[pltpu.VMEM((16, 8, HD), F32)],
        name="pack_queries",
    )(prefix_id, place, queries)


def pack_suffix_kernel(kv_ref, rows_ref, out_ref):
    for z in range(NZ):
        for y in range(NY):
            for r in range(2):
                for kind in range(2):
                    first = (2 * kind + r) * SPAN
                    block = kind * NZ + z
                    out_ref[y * NZ + z, first : first + SPAN, :] = kv_ref[
                        2 * y + r, :, block * HD : (block + 1) * HD
                    ]
            out_ref[y * NZ + z, 4 * SPAN :, :] = rows_ref[y]


def pack_suffix(suffix_kv, rows):
    return pl.pallas_call(
        pack_suffix_kernel,
        out_shape=jax.ShapeDtypeStruct((NZ * NY, MESSAGE, HD), BF16),
        in_specs=[pl.BlockSpec(memory_space=pltpu.VMEM)] * 2,
        out_specs=pl.BlockSpec(memory_space=pltpu.VMEM),
        compiler_params=pltpu.CompilerParams(vmem_limit_bytes=SMALL),
        name="pack_suffix",
    )(suffix_kv, rows)


def split_total(total):
    high = total.astype(BF16).astype(F32)
    return high, total - high


def lanes(block):
    return pl.ds(pl.multiple_of(block * HD, HD), HD)


def prefix_scores(queries, halves, z, p, score, peak):
    first = [pl.multiple_of((z * GRP + g) * 32 + p * 16, 16) for g in range(GRP)]
    q = jnp.concatenate([ref[pl.ds(row, 16), :] for ref in queries for row in first], axis=0)
    top = None
    for i, kv in enumerate(halves):
        for start in range(0, HALF, CHUNK):
            s = nt_dot(kv[p, start : start + CHUNK, lanes(z)], q)
            score[i * HALF + start : i * HALF + start + CHUNK, :] = s
            high = jnp.max(s.reshape(CHUNK // 8, 8, 256), axis=0)
            top = high if top is None else jnp.maximum(top, high)
    peak[...] = top


def prefix_values(halves, z, p, score, peak):
    top = jnp.max(peak[...], axis=0, keepdims=True) * FACTOR
    top = top.astype(BF16).astype(F32)
    total = jnp.zeros((8, 256), F32)
    summed = jnp.zeros((HD, 256), F32)
    for i, kv in enumerate(halves):
        for start in range(0, HALF, CHUNK):
            s = score[i * HALF + start : i * HALF + start + CHUNK, :]
            w = jnp.exp2(s * FACTOR - top)
            total = total + jnp.sum(w.reshape(CHUNK // 8, 8, 256), axis=0)
            v = kv[p, start : start + CHUNK, lanes(NZ + z)]
            summed = summed + tn_dot(v, w.astype(BF16))
    return summed, (top, jnp.sum(total, axis=0, keepdims=True))


def prefix_kernel(q0, q1, q2, q3, own, other, o0, o1, o2, o3, kv0, kv1, sa, sb, ma, mb, stats, sems):
    queries, halves = (q0, q1, q2, q3), (kv0, kv1)

    def fetch(half, kind, z):
        cols = lanes(kind * NZ + z)
        return pltpu.make_async_copy(
            (own, other)[half].at[:, :, cols], halves[half].at[:, :, cols], sems.at[half, kind, z]
        )

    for z in range(NZ):
        for kind in range(2):
            for half in range(2):
                fetch(half, kind, z).start()

    def ready(kind, z):
        fetch(0, kind, z).wait()
        fetch(1, kind, z).wait()

    def step(z, last):
        prefix_scores(queries, halves, z, 1, sb, mb)
        even = prefix_values(halves, z, 0, sa, ma)
        if not last:
            prefix_scores(queries, halves, z + 1, 0, sa, ma)
        odd = prefix_values(halves, z, 1, sb, mb)
        rows = pl.ds(pl.multiple_of(z * HD, HD), HD)
        for k, out in enumerate((o0, o1, o2, o3)):
            cols = slice(64 * k, 64 * (k + 1))
            out[rows, :] = jnp.concatenate([even[0][:, cols], odd[0][:, cols]], axis=1).astype(BF16)
            for i in range(2):
                stats[k, pl.ds(8 * i + z, 1), :] = jnp.concatenate(
                    [even[1][i][:, cols], odd[1][i][:, cols]], axis=1
                )

    stats[...] = jnp.zeros_like(stats)
    ready(0, 0)
    prefix_scores(queries, halves, 0, 0, sa, ma)

    def body(z, carry):
        ready(1, z)
        ready(0, z + 1)
        step(z, False)
        return carry

    lax.fori_loop(0, NZ - 1, body, 0)
    ready(1, NZ - 1)
    step(NZ - 1, True)
    for k, out in enumerate((o0, o1, o2, o3)):
        out[NZ * HD :, :] = stats[k].astype(BF16)


def prefix_attention(gathered, own, other):
    vmem = pl.BlockSpec(memory_space=pltpu.VMEM)
    hbm = pl.BlockSpec(memory_space=pl.ANY)
    return pl.pallas_call(
        prefix_kernel,
        out_shape=(jax.ShapeDtypeStruct((ROWS, HD), BF16),) * NY,
        in_specs=[vmem] * 4 + [hbm] * 2,
        out_specs=(vmem,) * NY,
        scratch_shapes=[
            pltpu.VMEM(own.shape, BF16),
            pltpu.VMEM(own.shape, BF16),
            pltpu.VMEM((2 * HALF, 256), F32),
            pltpu.VMEM((2 * HALF, 256), F32),
            pltpu.VMEM((8, 256), F32),
            pltpu.VMEM((8, 256), F32),
            pltpu.VMEM((NY, STATS, HD), F32),
            pltpu.SemaphoreType.DMA((2, 2, NZ)),
        ],
        compiler_params=pltpu.CompilerParams(vmem_limit_bytes=44 * 1024 * 1024),
        cost_estimate=pl.CostEstimate(
            flops=20 * 4096 * 2048 * HD, bytes_accessed=18 << 20, transcendentals=4096 * 2048
        ),
        name="prefix_attention",
    )(*gathered, own, other)


def suffix_kernel(len_ref, kv_own, kv_other, new_kv, o0, o1, o2, o3):
    y, z, core = lax.axis_index("y"), lax.axis_index("z"), lax.axis_index("c")
    index = lax.broadcasted_iota(jnp.int32, (32, 512), 1)
    source = index // SPAN
    base = (source % NZ * NY + source // NZ) * (2 * SPAN) + index % SPAN
    step = lax.broadcasted_iota(jnp.int32, (32, 1), 0) % STEPS
    sums, tops, totals = [], [], []
    queries = [
        kv_own[lax.rem(y + NY - k, NY) * NZ + z].astype(F32)[4 * SPAN :] for k in range(NY)
    ]
    for r in range(2):
        length = len_ref[2 * y + r]
        keys, values = slice(r * SPAN, (r + 1) * SPAN), slice((2 + r) * SPAN, (3 + r) * SPAN)
        qf = jnp.concatenate([q[8 * r : 8 * r + 8] for q in queries], axis=0)
        q = qf.astype(BF16)
        scores = []
        for ref, c in ((kv_own, core), (kv_other, 1 - core)):
            s = nt_dot(q, ref[:, keys, :].reshape(512, HD)) * FACTOR
            scores.append(jnp.where(base + c * SPAN < length, s, NEG))
        kn = new_kv[2 * y + r, :, lanes(z)].astype(F32)
        vn = new_kv[2 * y + r, :, lanes(NZ + z)].astype(F32)
        fresh = []
        for t in range(STEPS):
            s = jnp.sum(qf * kn[t : t + 1], axis=1, keepdims=True) * FACTOR
            fresh.append(jnp.where(step >= t, s, NEG))
        top = functools.reduce(
            jnp.maximum, [jnp.max(s, axis=1, keepdims=True) for s in scores] + fresh
        )
        top = top.astype(BF16).astype(F32)
        total = jnp.zeros((32, 1), F32)
        summed = jnp.zeros((32, HD), F32)
        for s, ref in zip(scores, (kv_own, kv_other)):
            w = jnp.exp2(s - top)
            total = total + jnp.sum(w, axis=1, keepdims=True)
            summed = summed + jnp.dot(
                w.astype(BF16), ref[:, values, :].reshape(512, HD), preferred_element_type=F32
            )
        for t in range(STEPS):
            w = jnp.exp2(fresh[t] - top)
            total = total + w
            summed = summed + w.astype(BF16).astype(F32) * vn[t : t + 1]
        sums.append(summed)
        tops.append(top)
        totals.append(total)
    lane = lax.broadcasted_iota(jnp.int32, (16, HD), 1)
    for k, out in enumerate((o0, o1, o2, o3)):
        rows = slice(8 * k, 8 * k + 8)
        top = jnp.concatenate([t[rows] for t in tops], axis=0)
        high, low = split_total(jnp.concatenate([t[rows] for t in totals], axis=0))
        out[:16, :] = jnp.concatenate([s[rows] for s in sums], axis=0).astype(BF16)
        stat = jnp.where(
            lane == 0, top, jnp.where(lane == 1, high, jnp.where(lane == 2, low, 0.0))
        )
        out[16:, :] = stat.astype(BF16)


def suffix_attention(lengths, kv_own, kv_other, new_kv):
    vmem = pl.BlockSpec(memory_space=pltpu.VMEM)
    return pl.pallas_call(
        suffix_kernel,
        in_specs=[pl.BlockSpec(memory_space=pltpu.SMEM)] + [vmem] * 3,
        out_specs=[vmem] * NY,
        out_shape=[jax.ShapeDtypeStruct((TAIL, HD), BF16)] * NY,
        cost_estimate=pl.CostEstimate(flops=1 << 20, bytes_accessed=1 << 16, transcendentals=0),
        compiler_params=pltpu.CompilerParams(vmem_limit_bytes=SMALL),
        name="suffix_attention",
    )(lengths, kv_own, kv_other, new_kv)


def combine_kernel(p0, p1, p2, p3, out_ref):
    stats = [ref[NZ * HD :, :].astype(F32) for ref in (p0, p1, p2, p3)]
    top = functools.reduce(jnp.maximum, [s[:NZ] for s in stats])
    factors = [jnp.exp2(s[:NZ] - top) for s in stats]
    total = sum(s[NZ : 2 * NZ] * f for s, f in zip(stats, factors))
    high, low = split_total(total)
    row = lax.broadcasted_iota(jnp.int32, (8, HD), 0)
    for z in range(NZ):
        at = slice(z, z + 1)
        rows = slice(z * HD, (z + 1) * HD)
        summed = sum(ref[rows].astype(F32) * f[at] for ref, f in zip((p0, p1, p2, p3), factors))
        stat = jnp.where(
            row == 0, top[at], jnp.where(row == 1, high[at], jnp.where(row == 2, low[at], 0.0))
        )
        turned = jnp.transpose(summed)
        for g in range(GRP):
            out_ref[z * GRP + g] = jnp.concatenate(
                [turned[16 * g : 16 * g + 16], turned[64 + 16 * g : 80 + 16 * g], stat], axis=0
            ).astype(BF16)


def combine(parts):
    spec = pl.BlockSpec(memory_space=pltpu.VMEM)
    return pl.pallas_call(
        combine_kernel,
        out_shape=jax.ShapeDtypeStruct((GRP * NZ, BACK, HD), BF16),
        in_specs=[spec] * 4,
        out_specs=spec,
        compiler_params=pltpu.CompilerParams(vmem_limit_bytes=SMALL),
        name="combine",
    )(*parts)


def finish_kernel(pid_ref, place_ref, back_ref, t0, t1, t2, t3, out_ref, turned, sums, tops, totals, tails):
    y, g = lax.axis_index("y"), lax.axis_index("grp")
    for k, ref in enumerate((t0, t1, t2, t3)):
        tails[k] = ref[...].astype(F32)
    blocks = [back_ref[s].astype(F32) for s in range(GRP * NZ)]
    rows = []
    for src in range(GRP):
        stats = [b[32:BACK] for b in blocks[src::GRP]]
        top = functools.reduce(jnp.maximum, [s[0:1] for s in stats])
        factors = [jnp.exp2(s[0:1] - top) for s in stats]
        total = sum((s[1:2] + s[2:3]) * f for s, f in zip(stats, factors))
        rows += factors + [top, total, jnp.zeros((6, HD), F32)]
    rows.append(jnp.zeros((64, HD), F32))
    turned[...] = jnp.transpose(jnp.concatenate(rows, axis=0))
    cols = jnp.concatenate(
        [
            turned[pl.ds(pl.multiple_of(16 * g, 16), 16), :],
            turned[pl.ds(pl.multiple_of(64 + 16 * g, 16), 16), :],
        ],
        axis=0,
    )
    for src in range(GRP):
        col = [cols[:, 16 * src + i : 16 * src + i + 1] for i in range(10)]
        summed = sum(blocks[z * GRP + src][:32] * col[z] for z in range(NZ))
        sums[4 * src : 4 * src + 4] = summed.reshape(4, 8, HD)
        tops[4 * src : 4 * src + 4] = jnp.broadcast_to(col[8], (32, HD)).reshape(4, 8, HD)
        totals[4 * src : 4 * src + 4] = jnp.broadcast_to(col[9], (32, HD)).reshape(4, 8, HD)
    for r in range(REQ):
        slot = slot_of(r, pid_ref, place_ref)
        k = (r // 2 + NY - y) % NY
        tail = tails[k]
        base = 8 * (r % 2)
        s_sum = tail[base : base + 8]
        stat = tail[16 + base : 24 + base]
        s_top, s_total = stat[:, 0:1], stat[:, 1:2] + stat[:, 2:3]
        p_sum, p_top, p_total = sums[slot], tops[slot], totals[slot]
        top = jnp.maximum(p_top, s_top)
        left, right = jnp.exp2(p_top - top), jnp.exp2(s_top - top)
        result = (p_sum * left + s_sum * right) / (p_total * left + s_total * right)
        out_ref[r] = jnp.concatenate([result[:STEPS], result[STEPS:]], axis=1).astype(BF16)


def finish(prefix_id, place, back, tails):
    smem, vmem = (pl.BlockSpec(memory_space=space) for space in (pltpu.SMEM, pltpu.VMEM))
    return pl.pallas_call(
        finish_kernel,
        out_shape=jax.ShapeDtypeStruct((REQ, STEPS, 2 * HD), BF16),
        in_specs=[smem, smem] + [vmem] * 5,
        out_specs=vmem,
        scratch_shapes=[
            pltpu.VMEM((HD, HD), F32),
            pltpu.VMEM((16, 8, HD), F32),
            pltpu.VMEM((16, 8, HD), F32),
            pltpu.VMEM((16, 8, HD), F32),
            pltpu.VMEM((NY, TAIL, HD), F32),
        ],
        compiler_params=pltpu.CompilerParams(vmem_limit_bytes=SMALL),
        name="finish",
    )(prefix_id, place, back, *tails)


def turn(x, by):
    return lax.ppermute(x, "y", [(i, (i + by) % NY) for i in range(NY)])


def swap(x):
    return lax.ppermute(x, "c", [(0, 1), (1, 0)])


def per_device(queries, prefix_kv, suffix_kv, new_kv, prefix_id, place, suffix_len):
    other_kv = swap(prefix_kv)
    prefix_id = prefix_id.reshape(REQ)
    send, rows = pack_queries(prefix_id, place, queries)
    packed = pack_suffix(suffix_kv, rows)
    arrived = lax.all_to_all(send, ("z", "grp"), 0, 0, tiled=True)
    arrived, other_kv = lax.optimization_barrier((arrived, other_kv))
    arrived = arrived.reshape(ARRIVED, HD)
    gathered = [arrived] + [turn(arrived, k) for k in range(1, NY)]
    suffix_own = lax.all_to_all(packed, ("y", "z"), 0, 0, tiled=True)
    partials = list(prefix_attention(gathered, prefix_kv, other_kv))
    suffix_own, partials[0] = lax.optimization_barrier((suffix_own, partials[0]))
    parts = [partials[0]] + [turn(partials[k], -k) for k in range(1, NY)]
    suffix_other = swap(suffix_own)
    tails = suffix_attention(suffix_len, suffix_own, suffix_other, new_kv)
    tails = [tails[0]] + [turn(tails[k], -k) for k in range(1, NY)]
    joined = combine(parts)
    back = lax.all_to_all(joined, ("z", "grp"), 0, 0, tiled=True)
    return finish(prefix_id, place, back, tails)


def solution(mesh):
    inner = Mesh(mesh.devices.reshape(GRP, NZ, NY, NC), ("grp", "z", "y", "c"))
    ctx = ("z", "y", "c")
    return jax.shard_map(
        per_device,
        mesh=inner,
        in_specs=(
            P("grp", None, ctx),
            P("grp", ctx, None),
            P("grp", ctx, None),
            P("grp", None, None),
            P("grp", None),
            P(),
            P("grp"),
        ),
        out_specs=P("grp", None, ctx),
        check_vma=False,
    )
```
